32 devices in a mesh: seq: 8 (over z, x), wt: 4 (over y, core).
Axes of the slice: x: 2, y: 2, z: 4, core: 2. Of those that a mesh axis runs over, the one named last changes fastest.
Arguments:
- tokens: bfloat16 [4, 1024, 2048], P('wt', 'seq'), may hold values from -6 to 6
- lengths: int32 [4], P('wt'), may hold values from 256 to 1024, as said below
- norm_gain: bfloat16 [2048], P('wt'), may hold values from 0.5 to 1.5
- in_weight: bfloat16 [2048, 8192], P('wt'), may hold values from -0.125 to 0.125
- conv_taps: bfloat16 [4, 4096], P(None, 'wt'), may hold values from -3 to 3
- conv_bias: bfloat16 [4096], P('wt'), may hold values from -2 to 2
- proj_weight: bfloat16 [4096, 160], P('wt'), may hold values from -0.09375 to 0.09375
- rate_weight: bfloat16 [128, 4096], P(None, 'wt'), may hold values from -0.5 to 0.5
- rate_bias: bfloat16 [4096], P('wt'), may hold values from -9 to -1
- skip_gain: bfloat16 [4096], P('wt'), may hold values from 0.5 to 1.5
- out_weight: bfloat16 [4096, 2048], P(None, 'wt'), may hold values from -0.1875 to 0.1875
- cotangent: bfloat16 [4, 1024, 2048], P('wt', 'seq'), may hold values from -6 to 6
Outputs:
- result: bfloat16 [4, 1024, 2048], P('wt', 'seq')
- grad_tokens: float32 [4, 1024, 2048], P('wt', 'seq')
- grad_gain: float32 [2048], P(('seq', 'wt'))
- grad_in: float32 [2048, 8192], P(('seq', 'wt'))
- grad_taps: float32 [4, 4096], P(None, ('seq', 'wt'))
- grad_conv_bias: float32 [4096], P(('seq', 'wt'))
- grad_proj: float32 [4096, 160], P(('seq', 'wt'))
- grad_rate: float32 [128, 4096], P(None, ('seq', 'wt'))
- grad_rate_bias: float32 [4096], P(('seq', 'wt'))
- grad_skip: float32 [4096], P(('seq', 'wt'))
- grad_out: float32 [4096, 2048], P(None, ('seq', 'wt'))
The draws below stay inside these ranges and needn't reach their ends.
Inputs may be any that keep to these rules, and one draw needn't show every extreme that they name: `lengths`: the valid positions of a sequence come first; one sequence has all 1024 positions valid and another 1024 // 4.
All inputs are finite; a program needn't handle non-finite values.
Results may differ from the reference program's by a relative error of at most 0.012.
The reference program's roundings to bfloat16 on the way count: a program that leaves them out, or rounds other values in their place, can miss the bound.
Values may be sent and summed in bfloat16 or wider, within the bound.
A program may use at most 320 MiB of HBM per device.

```python
import jax
import jax.numpy as jnp
from jax import lax

D = 2048
INNER = 4096
STATE = 16
CONV = 4
RANK = 128
BLOCK = 8
LEN = 1024
SEQ_ALL = 4


def draw_lengths(key, part):
    count = SEQ_ALL
    first, second, third = jax.random.split(key, 3)
    values = jax.random.randint(first, (count,), LEN // 4, LEN + 1)
    longest = jax.random.randint(second, (), 0, count)
    shortest = (longest + 1 + jax.random.randint(third, (), 0, max(count - 1, 1))) % count
    index = jnp.arange(count)
    values = jnp.where(index == longest, LEN, values)
    values = jnp.where(index == shortest, LEN // 4, values)
    return values.astype(jnp.int32)


def level_of(own_key, shape, cuts, smallest, top_value):
    level = 1.0
    for dim, parts in cuts:
        draws = jax.random.uniform(jax.random.fold_in(jax.random.fold_in(own_key, 6), dim), (parts,), jnp.float32, smallest / len(cuts), top_value / len(cuts))
        level = level * jnp.repeat(jnp.exp(draws), shape[dim] // parts).reshape((-1,) + (1,) * (len(shape) - 1 - dim))
    return level


def noise(stream_key, extent, width, limit, cuts=(), held_as=jnp.bfloat16):
    factor_of = level_of(stream_key, extent, cuts, -0.22, 0.18) if cuts else 1.0
    entries = jax.random.normal(stream_key, extent, jnp.float32) * width * factor_of
    return jnp.minimum(jnp.maximum(entries, -limit), limit).astype(held_as)


def setup_inputs(seed: int = 0) -> dict:
    splits = jax.random.split(jax.random.key(seed), 13)
    return {
        "tokens": noise(splits[0], (SEQ_ALL, LEN, D), 1.0, 6.0, ((0, 4), (1, 8))),
        "lengths": draw_lengths(jax.random.fold_in(splits[12], 71), 0),
        "norm_gain": jnp.clip(1.0 + 0.1 * jax.random.normal(splits[2], (D,), jnp.float32), 0.5, 1.5).astype(jnp.bfloat16),
        "in_weight": noise(splits[3], (D, 2 * INNER), D ** -0.5, 0.125, ((0, 4),)),
        "conv_taps": noise(splits[4], (CONV, INNER), 0.5, 3.0, ((1, 4),)),
        "conv_bias": noise(splits[5], (INNER,), 0.3, 2.0, ((0, 4),)),
        "proj_weight": noise(splits[6], (INNER, RANK + 2 * STATE), INNER ** -0.5, 0.09375, ((0, 4),)),
        "rate_weight": noise(splits[7], (RANK, INNER), RANK ** -0.5, 0.5, ((1, 4),)),
        "rate_bias": jnp.clip(-9.0 + 8.0 * jax.random.uniform(splits[8], (INNER,), jnp.float32) ** level_of(splits[8], (INNER,), ((0, 4),), -0.2, 0.2), -9.0, -1.0).astype(jnp.bfloat16),
        "skip_gain": jnp.clip(0.5 + 1.0 * jax.random.uniform(splits[9], (INNER,), jnp.float32) ** level_of(splits[9], (INNER,), ((0, 4),), -0.2, 0.2), 0.5, 1.5).astype(jnp.bfloat16),
        "out_weight": noise(splits[10], (INNER, D), (INNER // 4) ** -0.5, 0.1875, ((1, 4),)),
        "cotangent": noise(splits[11], (SEQ_ALL, LEN, D), 1.0, 6.0, ((0, 4), (1, 8))),
    }


EPS = 1e-05
HIGH = lax.Precision.HIGHEST

@jax.custom_vjp
def low(v):
    return lax.optimization_barrier(v.astype(jnp.bfloat16)).astype(jnp.float32)

@jax.custom_vjp
def low_back(v):
    return v

def low_keep(v):
    return (low(v), None)

def low_pass(kept, grad):
    return (grad,)

def back_keep(v):
    return (v, None)

def back_low(kept, grad):
    return (low(grad),)
low.defvjp(low_keep, low_pass)
low_back.defvjp(back_keep, back_low)

def matmul(left, right):
    return jnp.dot(left, right, precision=HIGH, preferred_element_type=jnp.float32)

def recurrence(inputs, rate_vals, key_vals, queries):

    def advance(state_now, member):
        input_row, rate_row, key_row, query_row = member
        key_norm = jnp.sum(key_row * key_row)
        denominator = 1.0 + rate_row * key_norm
        decay = (1.0 + rate_row[:, None] * (key_norm - key_row[None, :] * key_row[None, :])) / denominator[:, None]
        state_next = decay * state_now + (rate_row * input_row / denominator)[:, None] * key_row[None, :]
        return (state_next, lax.optimization_barrier(jnp.sum(state_next * query_row[None, :], axis=-1)))

    def run_block(state_now, members):
        return lax.scan(advance, state_now, members)
    blocked = tuple((array.reshape(LEN // BLOCK, BLOCK, array.shape[-1]) for array in (inputs, rate_vals, key_vals, queries)))
    zero_state = jnp.zeros((INNER, STATE), jnp.float32)
    _, outputs = lax.scan(jax.checkpoint(run_block), zero_state, blocked)
    return outputs.reshape(LEN, INNER)

def layer(tokens, valid_rows, norm_gain, in_weight, conv_taps, conv_bias, proj_weight, rate_weight, rate_bias, skip_gain, out_weight):
    inverse_rms = lax.rsqrt(lax.optimization_barrier(jnp.mean(tokens * tokens, axis=-1, keepdims=True)) + EPS)
    normed = low(tokens * inverse_rms * norm_gain)
    mixed_rows = low_back(low(matmul(normed, in_weight)))
    stream = mixed_rows[:, :INNER]
    gate_vals = mixed_rows[:, INNER:]
    padded = jnp.concatenate([jnp.zeros((CONV - 1, INNER), jnp.float32), stream], axis=0)
    summed = conv_bias
    for offset in range(CONV):
        summed = summed + conv_taps[offset] * padded[offset:offset + LEN]
    activated = low(jax.nn.silu(summed))
    projected = low(low_back(matmul(activated, proj_weight)))
    rate_in = projected[:, :RANK]
    key_vals = projected[:, RANK:RANK + STATE]
    queries = projected[:, RANK + STATE:]
    rate_vals = low(jax.nn.sigmoid(low_back(matmul(rate_in, rate_weight)) + rate_bias))
    scanned = low(recurrence(activated, rate_vals, key_vals, queries))
    gated = low((scanned + skip_gain * activated) * jax.nn.silu(gate_vals))
    return (tokens + matmul(gated, out_weight)) * valid_rows

def reference(tokens, lengths, norm_gain, in_weight, conv_taps, conv_bias, proj_weight, rate_weight, rate_bias, skip_gain, out_weight, cotangent):
    weights = tuple((weight.astype(jnp.float32) for weight in (norm_gain, in_weight, conv_taps, conv_bias, proj_weight, rate_weight, rate_bias, skip_gain, out_weight)))
    zero_grads = tuple((jnp.zeros(weight.shape, jnp.float32) for weight in weights))

    def one_sequence(totals, member):
        sequence, upstream, length = member
        valid_rows = (jnp.arange(LEN) < length).astype(jnp.float32)[:, None]

        def forward(inputs, *params):
            return layer(inputs, valid_rows, *params)
        output, pullback = jax.vjp(forward, sequence.astype(jnp.float32), *weights)
        gradients = pullback(upstream.astype(jnp.float32))
        totals = tuple((first + second for first, second in zip(totals, gradients[1:])))
        return (totals, (output.astype(jnp.bfloat16), gradients[0]))
    totals, (outputs, input_grads) = lax.scan(one_sequence, zero_grads, (tokens, cotangent, lengths))
    return (outputs, input_grads, totals[0], totals[1], totals[2], totals[3], totals[4], totals[5], totals[6], totals[7], totals[8])
```

```python
import functools

import jax
import jax.numpy as jnp
from jax import lax
from jax.experimental import pallas as pl
from jax.experimental.pallas import tpu as pltpu
from jax.sharding import PartitionSpec as P

EPS = 1e-05
f32 = jnp.float32
b16 = jnp.bfloat16


def own_lane(tall):
    row = lax.broadcasted_iota(jnp.int32, (tall, 128), 0)
    lane = lax.broadcasted_iota(jnp.int32, (tall, 128), 1)
    return (row == lane).astype(f32)


def spread_rows(kq_ref, first, wide):
    rows, tall, _ = wide.shape
    pick = own_lane(tall)
    picked = [(kq_ref[pl.ds(first + j, 1), :] * pick).astype(b16) for j in range(rows)]
    out = jnp.dot(jnp.concatenate(picked, 0), jnp.ones((128, 128), b16), preferred_element_type=f32)
    wide[...] = out.reshape(rows, tall, 128)


def gather_columns(sums):
    rows, tall, _ = sums.shape
    lane = lax.broadcasted_iota(jnp.int32, (tall, rows), 1)
    out = jnp.zeros((tall, rows), f32)
    for j in range(rows):
        out = jnp.where(lane == j, jnp.sum(sums[j], axis=1, keepdims=True), out)
    return out


def forward_rows(first, state, a_ref, u_ref, kqs, ys, h_ref, step=8):
    chunk, states, width = h_ref.shape
    groups = width // 128

    def body(i, h):
        base = pl.multiple_of(i * step, step)
        for j in range(step):
            t = base + j
            k = jnp.tile(kqs[t, :states], (1, groups))
            q = jnp.tile(kqs[t, states:], (1, groups))
            a = a_ref[pl.ds(first + t, 1), :]
            u = u_ref[pl.ds(first + t, 1), :]
            h_ref[t] = h.astype(b16)
            uk = u * k
            h = (1.0 - uk * k) * h + uk * a
            ys[pl.ds(first + t, 1), :] = jnp.sum(h * q, axis=0, keepdims=True)
        return h

    state[...] = lax.fori_loop(0, chunk // step, body, state[...])


def backward_rows(first, adjoint, after, a_ref, u_ref, g_ref, kqs, h_ref, ga_ref, gu_ref, sums, step=8):
    chunk, states, width = h_ref.shape
    groups = width // 128

    def fold(v):
        out = v[:, :128]
        for i in range(1, groups):
            out = out + v[:, i * 128:(i + 1) * 128]
        return out

    def body(i, carried):
        g, h_after = carried
        base = pl.multiple_of(chunk - step - i * step, step)
        for j in reversed(range(step)):
            t = base + j
            k = jnp.tile(kqs[t, :states], (1, groups))
            q = jnp.tile(kqs[t, states:], (1, groups))
            row = pl.ds(first + t, 1)
            a = a_ref[row, :]
            u = u_ref[row, :]
            gy = g_ref[row, :]
            h = h_ref[t].astype(f32)
            adj = gy * q + g
            sums[t, states:] = fold(gy * h_after)
            p = adj * k
            w = k * h
            d = a - w
            up = u * p
            sums[t, :states] = fold((u * adj) * (d - w))
            ga_ref[row, :] = jnp.sum(up, axis=0, keepdims=True)
            gu_ref[row, :] = jnp.sum(p * d, axis=0, keepdims=True)
            g = adj - k * up
            h_after = h
        return g, h_after

    g, h_after = lax.fori_loop(0, chunk // step, body, (adjoint[...], after[...]))
    adjoint[...] = g
    after[...] = h_after


def forward_all(chunk, segments, between, a_ref, u_ref, kq_ref, ys, h_full, state, kqs, hbuf, hsem, prepare):
    count = a_ref.shape[0] // chunk
    state[...] = jnp.zeros_like(state)

    def save(i):
        return pltpu.make_async_copy(hbuf.at[lax.rem(i, 2)], h_full.at[pl.ds(i * chunk, chunk)], hsem.at[lax.rem(i, 2)])

    def one(i, _):
        @pl.when(i >= 2)
        def _():
            save(i - 2).wait()
        first = pl.multiple_of(i * chunk, chunk)
        prepare(i)
        spread_rows(kq_ref, first, kqs)
        forward_rows(first, state, a_ref, u_ref, kqs, ys, hbuf.at[lax.rem(i, 2)])
        save(i).start()
        return 0

    for s in range(segments):
        lax.fori_loop(s * count // segments, (s + 1) * count // segments, one, 0)
        between()
    save(count - 2).wait()
    save(count - 1).wait()


MESH = pl.DeviceIdType.MESH
ANY = pl.BlockSpec(memory_space=pl.ANY)
IN_VMEM = pl.BlockSpec(memory_space=pltpu.VMEM)
MIB = 2**20


def remote(src, dst, sends, recvs, index, to):
    return pltpu.make_async_remote_copy(
        src_ref=src, dst_ref=dst, send_sem=sends.at[index], recv_sem=recvs.at[index],
        device_id=to, device_id_type=MESH)


class Place:
    def __init__(self, seq_count, wt_count):
        self.nx = 1 << ((seq_count.bit_length() - 1) // 2)
        self.nz = seq_count // self.nx
        self.nc = 2
        self.ny = wt_count // self.nc
        self.seq = lax.axis_index("seq")
        self.wt = lax.axis_index("wt")
        self.z = self.seq // self.nx
        self.x = lax.rem(self.seq, self.nx)
        self.y = self.wt // self.nc
        self.c = lax.rem(self.wt, self.nc)

    def z_at(self, d):
        return lax.rem(self.z + d + self.nz, self.nz)

    def x_at(self, d):
        return lax.rem(self.x + d + self.nx, self.nx)

    def y_at(self, d):
        return lax.rem(self.y + d + self.ny, self.ny)

    def to_z(self, d):
        return (self.z_at(d) * self.nx + self.x, self.wt)

    def to_x(self, d):
        return (self.z * self.nx + self.x_at(d), self.wt)

    def to_y(self, d):
        return (self.seq, self.y_at(d) * self.nc + self.c)

    def to_core(self):
        return (self.seq, self.y * self.nc + 1 - self.c)

    def to_seq(self, d):
        return (lax.rem(self.seq + d, self.nz * self.nx), self.wt)


def meet(peers):
    barrier = pltpu.get_barrier_semaphore()
    for to in peers:
        pl.semaphore_signal(barrier, inc=1, device_id=to, device_id_type=MESH)
    pl.semaphore_wait(barrier, len(peers))


def take_turns(tasks):
    tasks = list(tasks)
    while tasks:
        for task in list(tasks):
            try:
                next(task)
            except StopIteration:
                tasks.remove(task)


def gather_plane(at, own, full, parts, sems):
    zs, zr, xs, xr = sems
    copies = []
    for k in range(at.nz):
        slot = at.z_at(-k) * at.nx + at.x
        for h in range(parts):
            if k:
                remote(full.at[slot, h], full.at[slot, h], zs, zr, (k - 1, h), at.to_z(1)).wait_recv()
            src = full.at[slot, h] if k else own.at[h]
            if k < at.nz - 1:
                copy = remote(src, full.at[slot, h], zs, zr, (k, h), at.to_z(1))
                copy.start()
                copies.append(copy)
            for d in range(1, at.nx):
                copy = remote(src, full.at[slot, h], xs, xr, (k, d - 1, h), at.to_x(d))
                copy.start()
                copies.append(copy)
            yield
    for k in range(at.nz):
        for d in range(1, at.nx):
            slot = at.z_at(-k) * at.nx + at.x_at(-d)
            for h in range(parts):
                remote(full.at[slot, h], full.at[slot, h], xs, xr, (k, d - 1, h), at.to_x(d)).wait_recv()
                yield
    for copy in copies:
        copy.wait_send()


def gather_plane_sems(at_nz, at_nx, parts):
    dma = pltpu.SemaphoreType.DMA
    return [dma((at_nz, parts)), dma((at_nz, parts)),
            dma((at_nz, at_nx - 1, parts)), dma((at_nz, at_nx - 1, parts))]


def gather_wt(at, own, block, sems, rest=0):
    ys, yr, cs, cr = sems
    copies = []
    for d in range(1, at.ny):
        copy = remote(own, block(at.wt), ys, yr, (d,), at.to_y(d))
        copy.start()
        copies.append(copy)
    copy = remote(own, block(at.wt), cs, cr, (0,), at.to_core())
    copy.start()
    copies.append(copy)
    for _ in range(1 + rest):
        yield
    for d in range(1, at.ny):
        slot = at.y_at(-d) * at.nc + at.c
        remote(block(slot), block(slot), ys, yr, (d,), at.to_y(d)).wait_recv()
        copy = remote(block(slot), block(slot), cs, cr, (d,), at.to_core())
        copy.start()
        copies.append(copy)
        yield
    for d in range(at.ny):
        slot = at.y_at(-d) * at.nc + 1 - at.c
        remote(block(slot), block(slot), cs, cr, (d,), at.to_core()).wait_recv()
        yield
    for copy in copies:
        copy.wait_send()


def wt_sems(ny):
    return [pltpu.SemaphoreType.DMA((ny,)) for _ in range(4)]


def near(at, z=True, x=True, y=True, c=True):
    peers = []
    if z:
        peers += [at.to_z(1), at.to_z(-1)]
    if x:
        peers += [at.to_x(d) for d in range(1, at.nx)]
    if y:
        peers += [at.to_y(d) for d in range(1, at.ny)]
    if c:
        peers += [at.to_core()]
    return peers


def exchange_plane(at, send, recv, ss, rs, rest=0):
    count = at.nz * at.nx
    copies = []
    for d in range(1, count):
        to = lax.rem(at.seq + d, count)
        copy = remote(send.at[to], recv.at[at.seq], ss, rs, (d,), at.to_seq(d))
        copy.start()
        copies.append(copy)
    for _ in range(1 + rest):
        yield
    for d in range(1, count):
        slot = lax.rem(at.seq - d + count, count)
        remote(recv.at[slot], recv.at[slot], ss, rs, (d,), at.to_seq(d)).wait_recv()
    for copy in copies:
        copy.wait_send()


def turn(tasks):
    for task in list(tasks):
        try:
            next(task)
        except StopIteration:
            tasks.remove(task)


def grads_task(at, grad_part, cbuf, qbuf, ybuf, rbuf, abuf, grads_out, block_sems, move_sems, rest=0, hold=0):
    yield from reduce_block(at, grad_part, cbuf, qbuf, ybuf, rbuf, block_sems, rest)
    yield from exchange_plane(at, rbuf, abuf, *move_sems, rest=hold)
    width = rbuf.shape[-1]
    abuf[at.seq] = rbuf[at.seq]
    for s in range(abuf.shape[0]):
        grads_out[:, s * width:(s + 1) * width] = abuf[s].astype(f32)


def to_wt(at, d):
    count = at.ny * at.nc
    return (at.seq, lax.rem(at.wt + d + count, count))


def turns(tasks, count):
    for _ in range(count):
        turn(tasks)


def front_kernel(seq_count, wt_count, chunk, parts, *refs):
    refs = list(refs)

    def take(n):
        out = refs[:n]
        del refs[:n]
        return out

    own, gain_own, w_own, wo_own, pack_own, rate_own, proj_own, g_own = take(8)
    (n_out, w_out, wo_out, g_full, h_full, gate, pre, stream, act, y_ref, hend, sig, u_ref, kq_ref, projected,
     pack, w_rate, w_proj, inverse, gain) = take(20)
    n_full, w_full, wo_full, sbuf, ys, state, kqs, hbuf, part, psend, precv = take(11)
    hsem, local, gs, gr, ss, sr, s1, r1, s2, r2 = take(10)
    nsems, gsems, wsems = take(4), take(4), [take(4), take(4), take(4)]
    at = Place(seq_count, wt_count)
    rows, model = own.shape
    width = act.shape[1]
    rank = w_rate.shape[0]
    tall = kqs.shape[1]
    packs = 128 // tall
    lanes = gain_own.shape[1]
    owned = pack_own.shape[1]
    owner = at.seq * width // owned
    offset = pl.multiple_of(lax.rem(at.seq * width, owned), 128)
    taps = pack.shape[0] - 4

    pieces = [(pack_own.at[:, pl.ds(offset, width)], pack),
              (rate_own.at[:, pl.ds(offset, width)], w_rate),
              (proj_own.at[pl.ds(offset, width), :], w_proj)]
    halves = [w_own.at[:, pl.ds(pl.multiple_of(h * width * seq_count + at.seq * width, 128), width)] for h in range(2)]
    wo_mine = wo_own.at[pl.ds(pl.multiple_of(at.seq * width, 8), width), :]

    def wo_block(slot):
        return wo_full.at[:, pl.ds(pl.multiple_of(slot * lanes, 128), lanes)]

    mine = [pltpu.make_async_copy(halves[h], w_full.at[h, at.wt], local.at[h]) for h in range(2)]
    mine.append(pltpu.make_async_copy(wo_mine, wo_block(at.wt), local.at[3]))
    mine.append(pltpu.make_async_copy(g_own, g_full.at[at.seq], local.at[2]))
    for copy in mine:
        copy.start()
    gain[at.wt] = gain_own[...]
    sbuf[0:8, :] = jnp.zeros((8, width), f32)
    meet([at.to_seq(d) for d in range(1, seq_count)] + [to_wt(at, d) for d in range(1, wt_count)])

    gains = []
    for d in range(1, wt_count):
        copy = remote(gain.at[at.wt], gain.at[at.wt], gs, gr, (d,), to_wt(at, d))
        copy.start()
        gains.append(copy)
    weights = [gather_wt(at, halves[h], lambda slot, h=h: w_full.at[h, slot], wsems[h]) for h in range(2)]
    outward = [gather_wt(at, wo_mine, wo_block, wsems[2])]
    turn(weights)

    def piece_copy(i, d):
        src, dst = pieces[i]
        return pltpu.make_async_remote_copy(src_ref=src, dst_ref=dst, send_sem=ss.at[i, d], recv_sem=sr.at[i],
                                            device_id=to_wt(at, d), device_id_type=MESH)

    @pl.when(at.wt == owner)
    def _():
        for i in range(3):
            pltpu.make_async_copy(*pieces[i], ss.at[i, 0]).start()
            for d in range(1, wt_count):
                piece_copy(i, d).start()

    for d in range(1, wt_count):
        slot = lax.rem(at.wt - d + wt_count, wt_count)
        remote(gain.at[slot], gain.at[slot], gs, gr, (d,), to_wt(at, d)).wait_recv()

    high = rows // parts
    step = 16
    rowing = gather_plane(at, n_full.at[at.seq], n_full, parts, nsems)
    for h in range(parts):
        for i in range(0, high, step):
            at_rows = pl.ds(h * high + i, step)
            x = own[at_rows, :].astype(f32)
            inv = lax.rsqrt(jnp.mean(x * x, axis=-1, keepdims=True) + EPS)
            inverse[at_rows, :] = jnp.broadcast_to(inv, (step, 128))
            unit = x * inv
            for w in range(wt_count):
                n_full[at.seq, h, i:i + step, w * lanes:(w + 1) * lanes] = (
                    unit[:, w * lanes:(w + 1) * lanes] * gain[w]).astype(b16)
        next(rowing)
    turn(outward)
    for k in range(1, at.nz):
        for h in range(parts):
            next(rowing)
    going = [gather_plane(at, g_own, g_full, parts, gsems)]
    turns(going, parts)
    take_turns(weights)
    for copy in mine:
        copy.wait()

    @pl.when(at.wt == owner)
    def _():
        for i in range(3):
            pltpu.make_async_copy(*pieces[i], ss.at[i, 0]).wait()
            for d in range(1, wt_count):
                piece_copy(i, d).wait_send()

    @pl.when(at.wt != owner)
    def _():
        for i in range(3):
            piece_copy(i, 1).wait_recv()

    def mix(slot):
        block = n_full[slot].reshape(rows, model)
        first = pl.multiple_of(slot * rows, rows)
        for h in range(2):
            out = jnp.dot(block, w_full[h].reshape(model, width), preferred_element_type=f32).astype(b16)
            if h:
                gate[pl.ds(first, rows), :] = out
            else:
                stream[pl.ds(first, rows), :] = out
                sbuf[pl.ds(first + 8, rows), :] = out.astype(f32)

    for k in range(at.nz):
        mix(at.z_at(-k) * at.nx + at.x)
    for k in range(at.nz):
        for d in range(1, at.nx):
            for h in range(parts):
                next(rowing)
            mix(at.z_at(-k) * at.nx + at.x_at(-d))
    for _ in rowing:
        pass
    take_turns(outward)
    saves = [pltpu.make_async_copy(n_full, n_out, local.at[0]), pltpu.make_async_copy(w_full, w_out, local.at[1]),
             pltpu.make_async_copy(wo_full, wo_out, local.at[2])]
    for copy in saves:
        copy.start()
    turns(going, parts)

    first_sends = []
    bias = pack[taps:taps + 1, :]
    for d in list(range(1, seq_count)) + [0]:
        block = lax.rem(at.seq + d, seq_count)
        first = pl.multiple_of(block * rows, rows)
        total = bias
        window = sbuf[pl.ds(first, rows + 8), :]
        for j in range(taps):
            total = total + pack[j:j + 1, :] * window[9 - taps + j:9 - taps + j + rows]
        pre[pl.ds(first, rows), :] = total
        out = (total * jax.nn.sigmoid(total)).astype(b16)
        act[pl.ds(first, rows), :] = out.astype(f32)
        both = jnp.dot(out, w_proj[...], preferred_element_type=f32)
        part[d, :rank, :] = both[:, :rank]
        narrow = jnp.concatenate([both[:, rank:], jnp.zeros((rows, 128 - tall), f32)], axis=1)
        height = rows // packs
        packed = narrow[:height]
        for i in range(1, packs):
            packed = packed + pltpu.roll(narrow[i * height:(i + 1) * height], i * tall, axis=1)
        part[d, rank:, :] = packed
        if d:
            psend[d] = part[d].astype(b16)
            copy = remote(psend.at[d], precv.at[d], s1, r1, (d,), at.to_seq(d))
            copy.start()
            first_sends.append(copy)
    total = part[0]
    for d in range(1, seq_count):
        remote(precv.at[d], precv.at[d], s1, r1, (d,), at.to_seq(d)).wait_recv()
        total = total + precv[d].astype(f32)
    projected[at.seq] = total.astype(b16)
    second_sends = []
    for d in range(1, seq_count):
        copy = remote(projected.at[at.seq], projected.at[at.seq], s2, r2, (d,), at.to_seq(d))
        copy.start()
        second_sends.append(copy)
    for d in range(1, seq_count):
        slot = lax.rem(at.seq - d + seq_count, seq_count)
        remote(projected.at[slot], projected.at[slot], s2, r2, (d,), at.to_seq(d)).wait_recv()

    lane = lax.broadcasted_iota(jnp.int32, (rows, 128), 1)

    def prepare(i):
        first = pl.multiple_of(i * rows, rows)
        here = pl.ds(first, rows)
        packed = projected[i, rank:, :].astype(f32)
        kq = jnp.concatenate([packed] + [pltpu.roll(packed, 128 - j * tall, axis=1) for j in range(1, packs)], axis=0)
        kq_ref[here, :] = kq
        keys = jnp.where(lane < tall // 2, kq, 0.0)
        knorm = jnp.sum(keys * keys, axis=1, keepdims=True)
        s = jax.nn.sigmoid(jnp.dot(projected[i, :rank, :], w_rate[...], preferred_element_type=f32)
                           + pack[taps + 1:taps + 2, :])
        sig[here, :] = s
        rates = s.astype(b16).astype(f32)
        u_ref[here, :] = rates / (1.0 + rates * knorm)

    forward_all(chunk, min(8, seq_count), lambda: turn(going), act, u_ref, kq_ref, ys, h_full, state, kqs, hbuf, hsem,
                prepare)
    y_ref[...] = ys[...].astype(b16)
    hend[...] = state[...]
    take_turns(going)
    for copy in gains + first_sends + second_sends:
        copy.wait_send()
    for copy in saves:
        copy.wait()


def front(tokens, gain, in_weight, out_weight, pack, rate_weight, proj_weight, g_own, states, width, seq_count, wt_count, parts=2):
    rows, model = tokens.shape
    length = rows * seq_count
    rank = rate_weight.shape[0]
    tall = rank + 2 * states * rows // 128
    nx = 1 << ((seq_count.bit_length() - 1) // 2)
    nz = seq_count // nx
    split = (parts, rows // parts, model)
    vmem = pltpu.VMEM
    dma = pltpu.SemaphoreType.DMA

    def like(shape, dtype):
        return jax.ShapeDtypeStruct(shape, dtype)

    weights = (2, wt_count, model // wt_count, width)
    out = pl.pallas_call(
        functools.partial(front_kernel, seq_count, wt_count, rows, parts),
        in_specs=[IN_VMEM] * 2 + [ANY] * 6,
        out_specs=[ANY] * 5 + [IN_VMEM] * 15,
        out_shape=[like((seq_count,) + split, b16), like(weights, b16), like((width, model), b16),
                   like((seq_count,) + split, b16), like((length, states, width), b16),
                   like((length, width), b16), like((length, width), f32), like((length, width), b16),
                   like((length, width), f32), like((length, width), b16), like((states, width), f32),
                   like((length, width), f32), like((length, width), f32), like((length, 128), f32),
                   like((seq_count, tall, 128), b16), like((pack.shape[0], width), f32), like((rank, width), b16),
                   like((width, rank + 2 * states), b16), like((rows, 128), f32),
                   like((wt_count, 1, model // wt_count), f32)],
        scratch_shapes=[vmem((seq_count,) + split, b16), vmem(weights, b16), vmem((width, model), b16), vmem((8 + length, width), f32),
                        vmem((length, width), f32), vmem((states, width), f32), vmem((rows, 2 * states, 128), f32),
                        vmem((2, rows, states, width), b16), vmem((seq_count, tall, 128), f32),
                        vmem((seq_count, tall, 128), b16), vmem((seq_count, tall, 128), b16),
                        dma((2,)), dma((4,)), dma((wt_count,)), dma((wt_count,)), dma((3, wt_count)), dma((3,)),
                        dma((seq_count,)), dma((seq_count,)), dma((seq_count,)), dma((seq_count,))]
        + gather_plane_sems(nz, nx, parts) * 2 + wt_sems(wt_count // 2) * 3,
        compiler_params=pltpu.CompilerParams(collective_id=0, has_side_effects=True, vmem_limit_bytes=58 * MIB),
        name="front",
    )(tokens, gain, in_weight, out_weight, pack, rate_weight, proj_weight, g_own.reshape(split))
    return out


def add_rows(count, store, *terms):
    @pl.loop(0, count)
    def _(i):
        total = terms[0](i).astype(f32)
        for term in terms[1:]:
            total = total + term(i).astype(f32)
        store(i, total)


def reduce_block(at, part, cbuf, qbuf, ybuf, rbuf, sems, rest=0):
    cs, cr, ys, yr = sems
    count = part.shape[0]
    copies = []
    for d in range(at.ny):
        yd = at.y_at(d + 1)
        copy = remote(part.at[:, yd * at.nc + 1 - at.c], cbuf.at[d], cs, cr, (d,), at.to_core())
        copy.start()
        copies.append(copy)
    yield
    for d in range(at.ny):
        mine = at.y_at(d + 1) * at.nc + at.c
        remote(cbuf.at[d], cbuf.at[d], cs, cr, (d,), at.to_core()).wait_recv()
        if d < at.ny - 1:
            def store(i, total):
                qbuf[d, i] = total.astype(qbuf.dtype)
            add_rows(count, store, lambda i: part[i, mine], lambda i: cbuf[d, i])
            copy = remote(qbuf.at[d], ybuf.at[d], ys, yr, (d,), at.to_y(d + 1))
            copy.start()
            copies.append(copy)
            yield
    for _ in range(rest):
        yield
    for d in range(at.ny - 1):
        remote(ybuf.at[d], ybuf.at[d], ys, yr, (d,), at.to_y(d + 1)).wait_recv()

    def keep(i, total):
        rbuf[i] = total.astype(rbuf.dtype)
    add_rows(count, keep, lambda i: part[i, at.wt], lambda i: cbuf[at.ny - 1, i],
             *[lambda i, d=d: ybuf[d, i] for d in range(at.ny - 1)])
    for copy in copies:
        copy.wait_send()


def all_sum(at, box, wbox, sbox, sems):
    s1, r1, s2, r2 = sems
    copies = []
    others = [at.to_core()]
    for d in range(1, at.ny):
        others += [at.to_y(d), (at.seq, at.y_at(d) * at.nc + 1 - at.c)]
    for i, to in enumerate(others):
        copy = remote(box, wbox.at[i], s1, r1, (i,), to)
        copy.start()
        copies.append(copy)
    yield
    for i, copy in enumerate(copies):
        copy.wait()
    total = box[...]
    for i in range(len(others)):
        total = total + wbox[i]
    box[...] = total
    second = []
    count = at.nz * at.nx
    for d in range(1, count):
        copy = remote(box, sbox.at[d], s2, r2, (d,), at.to_seq(d))
        copy.start()
        second.append(copy)
    yield
    for copy in second:
        copy.wait()
    for d in range(1, count):
        total = total + sbox[d]
    box[...] = total


NT = (((1,), (1,)), ((), ()))
TN = (((0,), (0,)), ((), ()))


def dot_of(left, right, dims):
    return lax.dot_general(left, right, dims, preferred_element_type=f32)


def send(src, dst, send_sem, recv_sem, to):
    return pltpu.make_async_remote_copy(src_ref=src, dst_ref=dst, send_sem=send_sem, recv_sem=recv_sem,
                                        device_id=to, device_id_type=MESH)


def pack_rows(wide, narrow, tall):
    packs = 128 // tall
    height = narrow.shape[0] // packs
    packed = narrow[:height]
    for i in range(1, packs):
        packed = packed + pltpu.roll(narrow[i * height:(i + 1) * height], i * tall, axis=1)
    return jnp.concatenate([wide, packed], axis=0)


def unpack_rows(both, rows, tall):
    packed = both[rows:]
    return both[:rows], jnp.concatenate(
        [packed] + [pltpu.roll(packed, 128 - j * tall, axis=1) for j in range(1, 128 // tall)], axis=0)


def back_kernel(seq_count, wt_count, *refs):
    refs = list(refs)

    def take(n):
        out = refs[:n]
        del refs[:n]
        return out

    (a_in, u_in, gs_in, sig_in, pre_in, stream_in, gate_in, normed_in, h_in, wo_in, gated_in,
     kq_in, rate_in, last, early, w_in, w_rate, w_proj, pack, own, g_own, inverse, gain, valid) = take(24)
    tokens_out, stream_out, early_out, small_out, result_out, gain_out = take(6)
    adjoint, after, kqs, hbuf, sums, ga, gu, ebuf, four, three, nbuf, held, held16, window, accs = take(15)
    psend, precv, pown, proj = take(4)
    pbuf, xbuf, zbuf, acc, acc_rate, acc_proj, late, small = take(8)
    gx, total, wbuf, mypart, bbuf, box, wbox, sbox = take(8)
    grad_bufs = [take(5) for _ in range(3)]
    small_bufs = take(3)
    hsem, fsem, tsem, nsem, wsem, local, s1, r1, s2, r2, xs, xr, zs, zr, bs, br = take(16)
    gsems, gwsems = take(2), take(4)
    grad_sems = [take(6) for _ in range(3)]
    small_sems, sum_sems = take(4), take(4)

    at = Place(seq_count, wt_count)
    rows, model = own.shape
    width = u_in.shape[1]
    rank = w_rate.shape[0]
    states = adjoint.shape[0]
    tall = 2 * states
    half = hbuf.shape[1]
    slots = pbuf.shape[0]
    pieces = xs.shape[1]
    short = rows // pieces
    taps = pack.shape[0] - 4
    lanes = model // wt_count
    everyone = ([at.to_seq(d) for d in range(1, seq_count)] + [to_wt(at, d) for d in range(1, wt_count)])

    def load_four(b):
        slot = lax.rem(b, 2)
        return [pltpu.make_async_copy(src.at[pl.ds(b * rows, rows)], four.at[slot, i], fsem.at[slot, i])
                for i, src in enumerate((a_in, u_in, gs_in, sig_in))]

    def load_three(b):
        slot = lax.rem(b, 2)
        return ([pltpu.make_async_copy(pre_in.at[pl.ds(b * rows, rows)], window.at[slot], tsem.at[slot, 0])]
                + [pltpu.make_async_copy(src.at[pl.ds(b * rows, rows)], three.at[slot, i], tsem.at[slot, i + 1])
                   for i, src in enumerate((stream_in, gate_in))]
                + [pltpu.make_async_copy(normed_in.at[pl.ds(b * rows, rows)], nbuf.at[slot], nsem.at[slot])])

    def load_h(b, upper):
        return pltpu.make_async_copy(h_in.at[pl.ds(b * rows + upper * half, half)], hbuf.at[1 - upper],
                                     hsem.at[1 - upper])

    def start(copies):
        for copy in copies:
            copy.start()

    def wait(copies):
        for copy in copies:
            copy.wait()

    start(load_four(seq_count - 1))
    start(load_three(seq_count - 1))
    load_h(seq_count - 1, 1).start()
    mine = pltpu.make_async_copy(gated_in.at[at.seq], gx.at[at.wt, at.seq], local.at[0])
    mine.start()
    adjoint[...] = jnp.zeros_like(adjoint)
    after[...] = last[...]
    accs[...] = jnp.zeros_like(accs)
    box[...] = jnp.zeros_like(box)
    acc_rate[...] = jnp.zeros_like(acc_rate)
    acc_proj[...] = jnp.zeros_like(acc_proj)
    ahead = window.at[2]
    ahead[0:8, :] = jnp.zeros((8, width), f32)

    @pl.loop(0, model // 128)
    def _(i):
        acc[pl.ds(pl.multiple_of(i * 128, 128), 128), :] = jnp.zeros((128, width), f32)

    meet(everyone)

    def fetch(s):
        return pltpu.make_async_copy(wo_in.at[pl.ds(s * width, width)], wbuf.at[s % 2], wsem.at[s % 2])

    def product():
        yield from exchange_plane(at, gated_in, gx.at[at.wt], *gsems, rest=3)
        mine.wait()
        yield from gather_wt(at, gx.at[at.wt], lambda slot: gx.at[slot], gwsems, rest=3)
        fetch(0).start()
        for s in range(seq_count):
            if s + 1 < seq_count:
                fetch(s + 1).start()
            fetch(s).wait()
            for w in range(wt_count):
                term = jnp.dot(gx[w, s], wbuf[s % 2], preferred_element_type=f32)
                if s:
                    total[w] += term
                else:
                    total[w] = term
            if s % 2:
                yield
        copies = []
        for d in range(1, wt_count):
            to = lax.rem(at.wt + d, wt_count)
            copy = send(total.at[to], bbuf.at[at.wt], bs.at[d], br.at[d], to_wt(at, d))
            copy.start()
            copies.append(copy)
        bbuf[at.wt] = total[at.wt]
        yield
        yield
        for d in range(1, wt_count):
            slot = lax.rem(at.wt - d + wt_count, wt_count)
            send(bbuf.at[slot], bbuf.at[slot], bs.at[d], br.at[d], to_wt(at, d)).wait_recv()
        for w in range(wt_count):
            cols = slice(w * lanes, (w + 1) * lanes)
            result_out[:, cols] = ((own[:, cols].astype(f32) + bbuf[w]) * valid[...]).astype(b16)
        for copy in copies:
            copy.wait_send()

    tasks = [product()]
    for j in range(2):
        tasks.append(grads_task(at, early.at[j], *grad_bufs[j], early_out.at[j], grad_sems[j][:4], grad_sems[j][4:],
                                rest=2, hold=6))
    turn(tasks)
    turn(tasks[1:])

    lane = lax.broadcasted_iota(jnp.int32, (rows, 128), 1)

    def to_owner(b):
        return send(psend.at[b], precv.at[at.seq], s1.at[b], r1.at[at.seq], (b, at.wt))

    def from_other(b):
        return send(precv.at[b], precv.at[b], s1.at[b], r1.at[b], (b, at.wt))

    def to_all(d):
        return send(proj.at[at.seq], proj.at[at.seq], s2.at[d], r2.at[at.seq], at.to_seq(d))

    def from_owner(b):
        return send(proj.at[b], proj.at[b], s2.at[0], r2.at[b], (b, at.wt))

    def adjoint_block(b):
        slot = lax.rem(b, 2)

        @pl.when(b > 0)
        def _():
            start(load_four(b - 1))
        wait(load_four(b))
        a, u, gs, sig = (four.at[slot, i] for i in range(4))
        for upper in (1, 0):
            spread_rows(kq_in, pl.multiple_of(b * rows + upper * half, half), kqs)
            if upper:
                load_h(b, 0).start()
            else:
                @pl.when(b > 0)
                def _():
                    load_h(b - 1, 1).start()
            load_h(b, upper).wait()
            backward_rows(upper * half, adjoint, after, a, u, gs, kqs, hbuf.at[1 - upper], ga, gu, sums)
            ebuf[:, upper * half:(upper + 1) * half] = gather_columns(sums)
        keys = jnp.where(lane < states, kq_in[pl.ds(pl.multiple_of(b * rows, rows), rows), :], 0.0)
        knorm = jnp.sum(keys * keys, axis=1, keepdims=True)
        s = sig[...]
        den = 1.0 + s.astype(b16).astype(f32) * knorm
        g_u = gu[...]
        g_pre = g_u / (den * den) * s * (1.0 - s)
        u_all = u[...]
        g_knorm = -jnp.sum(g_u * u_all * u_all, axis=1, keepdims=True)
        accs[taps + 1:taps + 2, :] += jnp.sum(g_pre, axis=0, keepdims=True)
        accs[taps + 2:taps + 3, :] += jnp.sum(gs[...] * a[...], axis=0, keepdims=True)
        g16 = g_pre.astype(b16)
        acc_rate[...] += dot_of(rate_in[b], g16, TN)
        sums_t = jnp.transpose(jnp.concatenate([ebuf[...], jnp.zeros((128 - tall, rows), f32)], axis=0))
        payload = pack_rows(dot_of(g16, w_rate[...], NT), sums_t + 2.0 * keys * g_knorm, tall)
        held[lax.rem(b, 3)] = ga[...] + gs[...] * pack[taps + 2:taps + 3, :]
        held16[lax.rem(b, 3)] = a[...].astype(b16)

        @pl.when(b != at.seq)
        def _():
            psend[b] = payload.astype(b16)
            to_owner(b).start()

        @pl.when(b == at.seq)
        def _():
            pown[...] = payload

    def sum_block(b):
        @pl.when(b == at.seq)
        def _():
            for d in range(1, seq_count):
                other = lax.rem(at.seq + d, seq_count)
                from_other(other).wait_recv()
                pown[...] += precv[other].astype(f32)
            proj[at.seq] = pown[...].astype(b16)
            for d in range(1, seq_count):
                to_all(d).start()

    def kept(b):
        return lax.rem(b, slots) if slots < seq_count else b

    def piece(p):
        return pl.ds(p * short, short)

    def to_column(b, p):
        zb, xb = b // at.nx, lax.rem(b, at.nx)
        place = lax.rem(at.x - xb + at.nx, at.nx) - 1
        return send(pbuf.at[kept(b), piece(p)], xbuf.at[zb, place, piece(p)], xs.at[kept(b), p],
                    xr.at[zb, place, p], (at.z * at.nx + xb, at.wt))

    def onward(b, p, down):
        zb = b // at.nx
        z = at.z - 1 if down else at.z + 1
        slot = jnp.where(z == zb, at.nz, zb) if down else zb
        return send(pbuf.at[kept(b), piece(p)], zbuf.at[slot, piece(p)], zs.at[kept(b), p], zr.at[slot, p],
                    (z * at.nx + at.x, at.wt))

    def wait_sent(b):
        zb, xb = b // at.nx, lax.rem(b, at.nx)

        @pl.when(at.x != xb)
        def _():
            for p in range(pieces):
                to_column(b, p).wait_send()

        @pl.when((at.x == xb) & (zb > at.z))
        def _():
            for p in range(pieces):
                onward(b, p, False).wait_send()

        @pl.when((at.x == xb) & (zb < at.z))
        def _():
            for p in range(pieces):
                onward(b, p, True).wait_send()

    def conv_block(b):
        slot = lax.rem(b, 2)

        @pl.when(b > 0)
        def _():
            start(load_three(b - 1))

        @pl.when(b != at.seq)
        def _():
            from_owner(b).wait_recv()
        wait(load_three(b))
        wide, narrow = unpack_rows(proj[b].astype(f32), rows, tall)
        narrow = jnp.where(lane < tall, narrow, 0.0)
        wide16, narrow16 = wide.astype(b16), narrow.astype(b16)
        act16 = held16[lax.rem(b, 3)]
        g_act = (dot_of(wide16, w_proj[:, :rank], NT) + dot_of(narrow16[:, :tall], w_proj[:, rank:], NT)
                 + held[lax.rem(b, 3)])
        turned = jnp.concatenate([jnp.transpose(wide), jnp.transpose(narrow)[:tall]], axis=0).astype(b16)
        acc_proj[...] += jnp.dot(turned, act16, preferred_element_type=f32)
        pre = window[slot]
        s = jax.nn.sigmoid(pre)
        g_pre = g_act * s * (1.0 + pre * (1.0 - s))
        wider = jnp.concatenate([g_pre, ahead[0:8, :]], axis=0)
        ahead[0:8, :] = g_pre[0:8]
        accs[taps:taps + 1, :] += jnp.sum(g_pre, axis=0, keepdims=True)
        stream = three[slot, 0].astype(f32)
        g_stream = 0.0
        for j in range(taps):
            moved = wider[taps - 1 - j:taps - 1 - j + rows]
            g_stream = g_stream + pack[j:j + 1, :] * moved
            accs[j:j + 1, :] += jnp.sum(moved * stream, axis=0, keepdims=True)
        g16 = g_stream.astype(b16)
        g_gate = three[slot, 1]
        if slots < seq_count:
            @pl.when(b + slots < seq_count)
            def _():
                wait_sent(b + slots)
        for m in range(0, model, lanes):
            cols = slice(m, m + lanes)
            g_normed = dot_of(g16, w_in[0, cols, :], NT) + dot_of(g_gate, w_in[1, cols, :], NT)
            box[:, cols] += jnp.sum(g_normed * nbuf[slot, :, cols].astype(f32), axis=0, keepdims=True)
            pbuf[kept(b), :, cols] = g_normed.astype(b16)

        @pl.when(b == at.seq)
        def _():
            mypart[...] = pbuf[kept(b)]

        @pl.when(at.x != lax.rem(b, at.nx))
        def _():
            for p in range(pieces):
                to_column(b, p).start()
        for m in range(0, model, 256):
            acc[m:m + 256, :] += dot_of(nbuf[slot, :, m:m + 256], g16, TN)

    def from_column(b, place, p):
        zb = b // at.nx
        return send(xbuf.at[zb, place, piece(p)], xbuf.at[zb, place, piece(p)], xs.at[0, p], xr.at[zb, place, p],
                    (at.seq, at.wt))

    def arrived(slot, p):
        return send(zbuf.at[slot, piece(p)], zbuf.at[slot, piece(p)], zs.at[0, p], zr.at[slot, p], (at.seq, at.wt))

    step = 16

    def add_column(b, p, base, store, sources):
        zb = b // at.nx
        for place in range(at.nx - 1):
            from_column(b, place, p).wait_recv()
        for slot, there in sources:
            @pl.when(there)
            def _():
                arrived(slot, p).wait_recv()
        for i in range(0, short, step):
            here = pl.ds(p * short + i, step)
            value = base(here).astype(f32)
            for place in range(at.nx - 1):
                value = value + xbuf[zb, place, here, :].astype(f32)
            for slot, there in sources:
                value = value + jnp.where(there, zbuf[slot, here, :].astype(f32), 0.0)
            store(here, value)

    def pass_block(b, hops):
        zb, xb = b // at.nx, lax.rem(b, at.nx)

        @pl.when((at.x == xb) & (((zb > at.z) & (at.z == hops)) | ((zb < at.z) & (at.nz - 1 - at.z == hops))))
        def _():
            def store(here, value):
                pbuf[kept(b), here, :] = value.astype(b16)
            for p in range(pieces):
                add_column(b, p, lambda here: pbuf[kept(b), here, :], store, [(zb, hops > 0)] if hops else [])

                @pl.when(zb > at.z)
                def _():
                    onward(b, p, False).start()

                @pl.when(zb < at.z)
                def _():
                    onward(b, p, True).start()

    def each(i, _):
        b = seq_count - 1 - i

        @pl.when(b >= 0)
        def _():
            adjoint_block(b)

        @pl.when((b + 1 >= 0) & (b + 1 < seq_count))
        def _():
            sum_block(b + 1)

        @pl.when((b + 2 >= 0) & (b + 2 < seq_count))
        def _():
            conv_block(b + 2)
        for hops in range(at.nz - 1):
            later = b + 3 + 2 * hops

            @pl.when((later >= 0) & (later < seq_count))
            def _():
                pass_block(later, hops)
        return 0

    segments = min(8, seq_count)
    for s in range(segments):
        lax.fori_loop(s * seq_count // segments, (s + 1) * seq_count // segments, each, 0)
        turn(tasks)
    lax.fori_loop(seq_count, seq_count + 2, each, 0)

    @pl.loop(0, seq_count)
    def _(i):
        for w in range(wt_count):
            high = late.shape[2]
            at_row = pl.multiple_of(i * (wt_count * high) + w * high, high)
            late[i, w] = acc[pl.ds(at_row, high), :].astype(b16)

    thin = width // wt_count
    for w in range(wt_count):
        cols = slice(w * thin, (w + 1) * thin)
        small[0, w, :rank] = acc_rate[:, cols]
        small[0, w, rank:rank + rank + tall] = acc_proj[:, cols]
        small[0, w, rank + rank + tall:] = accs[:, cols]
    tasks.append(grads_task(at, late, *grad_bufs[2], stream_out, grad_sems[2][:4], grad_sems[2][4:], hold=4))
    tasks.append(reduce_block(at, small, *small_bufs, small_out, small_sems))
    box[...] = box[...] / gain[...]
    tasks.append(all_sum(at, box, wbox, sbox, sum_sems))
    turn(tasks)
    lax.fori_loop(seq_count + 2, seq_count + 3, each, 0)
    turn(tasks)
    lax.fori_loop(seq_count + 3, seq_count + 3 + 2 * (at.nz - 2), each, 0)

    def emit(here, g):
        own_rows = own[here, :].astype(f32)
        inv = inverse[here, :]
        scaled = g * gain[...]
        mean = jnp.mean(scaled * own_rows, axis=-1, keepdims=True)
        tokens_out[here, :] = (g_own[here, :].astype(f32) + inv * scaled
                               - own_rows * (inv * inv * inv) * mean)

    def rest():
        for p in range(pieces):
            add_column(at.seq, p, lambda here: mypart[here, :], emit,
                       [(at.z, at.z > 0), (at.nz, at.z < at.nz - 1)])
            yield

    tasks.append(rest())
    take_turns(tasks)
    gain_out[...] = box[...]

    @pl.loop(0, seq_count)
    def _(b):
        @pl.when(b != at.seq)
        def _():
            to_owner(b).wait_send()

    @pl.loop(0, slots)
    def _(b):
        wait_sent(b)
    for d in range(1, seq_count):
        to_all(d).wait_send()


def back(arrays, kq, rate_in, last, early, w_in, w_rate, w_proj, pack, own, g_own, inverse, gain, valid,
         seq_count, wt_count):
    gated = arrays[-1]
    rows, model = own.shape
    width = gated.shape[-1]
    states = last.shape[0]
    tall = 2 * states
    rank = w_rate.shape[0]
    high = early.shape[-2]
    half = rows // 2
    nx = 1 << ((seq_count.bit_length() - 1) // 2)
    nz = seq_count // nx
    ny = wt_count // 2
    taps = pack.shape[0] - 4
    payload = (rank + tall * rows // 128, 128)
    block = (seq_count, high, width)
    lanes = model // wt_count
    small_rows = 2 * rank + tall + 8
    small_block = (1, small_rows, width // wt_count)
    y_less = max(ny - 1, 1)
    vmem = pltpu.VMEM
    dma = pltpu.SemaphoreType.DMA

    def like(shape, dtype):
        return jax.ShapeDtypeStruct(shape, dtype)

    block_bufs = [vmem((ny,) + block, b16), vmem((y_less,) + block, b16), vmem((y_less,) + block, b16),
                  vmem(block, b16), vmem(block, b16)]
    small_bufs = [vmem((ny,) + small_block, f32), vmem((y_less,) + small_block, f32), vmem((y_less,) + small_block, f32)]
    return pl.pallas_call(
        functools.partial(back_kernel, seq_count, wt_count),
        in_specs=[ANY] * 11 + [IN_VMEM] * 13,
        out_specs=[IN_VMEM] * 6,
        out_shape=[like((rows, model), f32), like((high, seq_count * width), f32), like((2, high, seq_count * width), f32),
                   like(small_block, f32), like((rows, model), b16), like((1, model), f32)],
        scratch_shapes=[vmem((states, width), f32), vmem((states, width), f32), vmem((half, tall, 128), f32),
                        vmem((2, half, states, width), b16), vmem((half, tall, 128), f32),
                        vmem((rows, width), f32), vmem((rows, width), f32), vmem((tall, rows), f32),
                        vmem((2, 4, rows, width), f32), vmem((2, 2, rows, width), b16), vmem((2, rows, model), b16),
                        vmem((3, rows, width), f32), vmem((3, rows, width), b16), vmem((3, rows, width), f32),
                        vmem((8, width), f32),
                        vmem((seq_count,) + payload, b16), vmem((seq_count,) + payload, b16), vmem(payload, f32),
                        vmem((seq_count,) + payload, b16),
                        vmem((min(seq_count, 16), rows, model), b16), vmem((nz, nx - 1, rows, model), b16),
                        vmem((nz + 1, rows, model), b16), vmem((model, width), f32), vmem((rank, width), f32),
                        vmem((rank + tall, width), f32), vmem((seq_count, wt_count, high, width), b16),
                        vmem((1, wt_count) + small_block[1:], f32),
                        vmem((wt_count, seq_count, rows, width), b16), vmem((wt_count, rows, lanes), f32),
                        vmem((2, width, lanes), b16), vmem((rows, model), b16), vmem((wt_count, rows, lanes), f32),
                        vmem((1, model), f32), vmem((wt_count - 1, 1, model), f32), vmem((seq_count, 1, model), f32)]
        + block_bufs * 3 + small_bufs
        + [dma((2,)), dma((2, 4)), dma((2, 3)), dma((2,)), dma((2,)), dma((1,))] + [dma((seq_count,))] * 4
        + [dma((min(seq_count, 16), 4)), dma((nz, nx - 1, 4)), dma((min(seq_count, 16), 4)), dma((nz + 1, 4)), dma((wt_count,)), dma((wt_count,))]
        + [dma((seq_count,))] * 2 + [dma((ny,))] * 4
        + ([dma((ny,))] * 4 + [dma((seq_count,))] * 2) * 3
        + [dma((ny,))] * 4 + [dma((wt_count - 1,))] * 2 + [dma((seq_count,))] * 2,
        compiler_params=pltpu.CompilerParams(collective_id=5, has_side_effects=True, vmem_limit_bytes=62 * MIB),
        name="back",
    )(*arrays, kq, rate_in, last, early, w_in, w_rate, w_proj, pack, own, g_own, inverse, gain, valid)


def silu_parts(v):
    s = jax.nn.sigmoid(v)
    return v * s, s * (1.0 + v * (1.0 - s))


def on_device(
    tokens,
    lengths,
    norm_gain,
    in_weight,
    conv_taps,
    conv_bias,
    proj_weight,
    rate_weight,
    rate_bias,
    skip_gain,
    out_weight,
    cotangent,
):
    num_seqs, piece_len, model_width = tokens.shape
    inner_width = out_weight.shape[0]
    rate_rank = rate_weight.shape[0]
    states = (proj_weight.shape[1] - rate_rank) // 2
    conv_len = conv_taps.shape[0]
    seq_count = lax.axis_size("seq")
    wt_count = lax.axis_size("wt")
    length = piece_len * seq_count
    rows = num_seqs * length
    own_rows = num_seqs * piece_len
    width = inner_width // seq_count
    place = lax.axis_index("seq")

    own = tokens.reshape(own_rows, model_width)
    positions = place * piece_len + jnp.arange(piece_len, dtype=jnp.int32)
    valid = (positions[None, :] < lengths[:, None]).astype(f32).reshape(own_rows, 1)
    g_own16 = (cotangent.reshape(own_rows, model_width).astype(f32) * valid).astype(b16)
    pack = jnp.concatenate(
        [conv_taps] + [v[None] for v in (conv_bias, rate_bias, skip_gain, skip_gain)], 0).astype(f32)
    (normed, w_in, w_out, g_out, held, gate16, pre, stream16, act, scanned16, last, sig, u, key_query, projected,
     pack, w_rate, w_proj, inverse_rms, gain) = front(
        own, norm_gain.astype(f32).reshape(1, -1), in_weight, out_weight, pack, rate_weight, proj_weight, g_own16,
        states, width, seq_count, wt_count)
    normed = normed.reshape(rows, model_width)
    g_out = g_out.reshape(rows, model_width)
    w_in = w_in.reshape(2, model_width, width)
    inverse_rms = inverse_rms[:, :1]
    gain = gain.reshape(1, model_width)
    taps = pack[:conv_len]
    skip = pack[conv_len + 2][None]
    gate = gate16.astype(f32)
    rate_in = projected[:, :rate_rank]

    g_gated = jnp.einsum("td,id->ti", g_out, w_out, preferred_element_type=f32)
    gate_silu, gate_slope = silu_parts(gate)
    g_scanned = g_gated * gate_silu
    mixer = scanned16.astype(f32) + skip * act
    gated16 = (mixer * gate_silu).astype(b16)
    g_gate16 = (g_gated * mixer * gate_slope).astype(b16)
    part_out = jnp.einsum("td,ti->di", g_out, gated16, preferred_element_type=f32).astype(b16)
    part_gate = jnp.einsum("td,tk->dk", normed, g_gate16, preferred_element_type=f32).astype(b16)

    def by_owner(array):
        return array.reshape(array.shape[:-2] + (seq_count, wt_count, -1, width))

    grad_tokens, stream_part, early, packed, result, grad_gain = back(
        (act, u, g_scanned, sig, pre, stream16, g_gate16, normed, held, out_weight,
         gated16.reshape(seq_count, own_rows, width)),
        key_query, rate_in, last, by_owner(jnp.stack([part_gate, part_out])), w_in, w_rate, w_proj, pack,
        own, g_own16, inverse_rms, gain, valid, seq_count, wt_count)
    result = result.reshape(tokens.shape)
    inw_own = jnp.concatenate([stream_part, early[0]], axis=1)
    grad_tokens = grad_tokens.reshape(tokens.shape)
    outw_own = early[1].T
    owner = place * wt_count + lax.axis_index("wt")
    gain_own = lax.dynamic_slice_in_dim(grad_gain[0], owner * inw_own.shape[0], inw_own.shape[0], 0)
    packed = packed[0]
    ratew_own = packed[:rate_rank]
    at = rate_rank + proj_weight.shape[1]
    projw_own = packed[rate_rank:at].T
    taps_own = packed[at:at + conv_len]
    cbias_own, rbias_own, skip_own = (packed[at + conv_len + i] for i in range(3))
    return (
        result,
        grad_tokens,
        gain_own,
        inw_own,
        taps_own,
        cbias_own,
        projw_own,
        ratew_own,
        rbias_own,
        skip_own,
        outw_own,
    )


def solution(mesh):
    in_specs = (
        P("wt", "seq", None),
        P("wt"),
        P("wt"),
        P("wt", None),
        P(None, "wt"),
        P("wt"),
        P("wt", None),
        P(None, "wt"),
        P("wt"),
        P("wt"),
        P(None, "wt"),
        P("wt", "seq", None),
    )
    out_specs = (
        P("wt", "seq", None),
        P("wt", "seq", None),
        P(("seq", "wt")),
        P(("seq", "wt"), None),
        P(None, ("seq", "wt")),
        P(("seq", "wt")),
        P(("seq", "wt"), None),
        P(None, ("seq", "wt")),
        P(("seq", "wt")),
        P(("seq", "wt")),
        P(None, ("seq", "wt")),
    )
    return jax.shard_map(
        on_device, mesh=mesh, in_specs=in_specs, out_specs=out_specs, check_vma=False
    )
```

```python
import functools

import jax
import jax.numpy as jnp
from jax import lax
from jax.experimental import pallas as pl
from jax.experimental.pallas import tpu as pltpu
from jax.sharding import PartitionSpec as P

EPS = 1e-05
f32 = jnp.float32
b16 = jnp.bfloat16


def own_lane(tall):
    row = lax.broadcasted_iota(jnp.int32, (tall, 128), 0)
    lane = lax.broadcasted_iota(jnp.int32, (tall, 128), 1)
    return (row == lane).astype(f32)


def spread_rows(kq_ref, first, wide):
    rows, tall, _ = wide.shape
    pick = own_lane(tall)
    picked = [(kq_ref[pl.ds(first + j, 1), :] * pick).astype(b16) for j in range(rows)]
    out = jnp.dot(jnp.concatenate(picked, 0), jnp.ones((128, 128), b16), preferred_element_type=f32)
    wide[...] = out.reshape(rows, tall, 128)


def gather_columns(sums):
    rows, tall, _ = sums.shape
    lane = lax.broadcasted_iota(jnp.int32, (tall, rows), 1)
    out = jnp.zeros((tall, rows), f32)
    for j in range(rows):
        out = jnp.where(lane == j, jnp.sum(sums[j], axis=1, keepdims=True), out)
    return out


def forward_rows(first, state, a_ref, u_ref, kqs, ys, h_ref, step=8):
    chunk, states, width = h_ref.shape
    groups = width // 128

    def body(i, h):
        base = pl.multiple_of(i * step, step)
        for j in range(step):
            t = base + j
            k = jnp.tile(kqs[t, :states], (1, groups))
            q = jnp.tile(kqs[t, states:], (1, groups))
            a = a_ref[pl.ds(first + t, 1), :]
            u = u_ref[pl.ds(first + t, 1), :]
            h_ref[t] = h.astype(b16)
            uk = u * k
            h = (1.0 - uk * k) * h + uk * a
            ys[pl.ds(first + t, 1), :] = jnp.sum(h * q, axis=0, keepdims=True)
        return h

    state[...] = lax.fori_loop(0, chunk // step, body, state[...])


def backward_rows(first, adjoint, after, a_ref, u_ref, g_ref, kqs, h_ref, ga_ref, gu_ref, sums, step=8):
    chunk, states, width = h_ref.shape
    groups = width // 128

    def fold(v):
        out = v[:, :128]
        for i in range(1, groups):
            out = out + v[:, i * 128:(i + 1) * 128]
        return out

    def body(i, carried):
        g, h_after = carried
        base = pl.multiple_of(chunk - step - i * step, step)
        for j in reversed(range(step)):
            t = base + j
            k = jnp.tile(kqs[t, :states], (1, groups))
            q = jnp.tile(kqs[t, states:], (1, groups))
            row = pl.ds(first + t, 1)
            a = a_ref[row, :]
            u = u_ref[row, :]
            gy = g_ref[row, :]
            h = h_ref[t].astype(f32)
            adj = gy * q + g
            sums[t, states:] = fold(gy * h_after)
            p = adj * k
            w = k * h
            d = a - w
            up = u * p
            sums[t, :states] = fold((u * adj) * (d - w))
            ga_ref[row, :] = jnp.sum(up, axis=0, keepdims=True)
            gu_ref[row, :] = jnp.sum(p * d, axis=0, keepdims=True)
            g = adj - k * up
            h_after = h
        return g, h_after

    g, h_after = lax.fori_loop(0, chunk // step, body, (adjoint[...], after[...]))
    adjoint[...] = g
    after[...] = h_after


def forward_all(chunk, segments, between, a_ref, u_ref, kq_ref, ys, h_full, state, kqs, hbuf, hsem, prepare):
    count = a_ref.shape[0] // chunk
    state[...] = jnp.zeros_like(state)

    def save(i):
        return pltpu.make_async_copy(hbuf.at[lax.rem(i, 2)], h_full.at[pl.ds(i * chunk, chunk)], hsem.at[lax.rem(i, 2)])

    def one(i, _):
        @pl.when(i >= 2)
        def _():
            save(i - 2).wait()
        first = pl.multiple_of(i * chunk, chunk)
        prepare(i)
        spread_rows(kq_ref, first, kqs)
        forward_rows(first, state, a_ref, u_ref, kqs, ys, hbuf.at[lax.rem(i, 2)])
        save(i).start()
        return 0

    for s in range(segments):
        lax.fori_loop(s * count // segments, (s + 1) * count // segments, one, 0)
        between()
    save(count - 2).wait()
    save(count - 1).wait()


MESH = pl.DeviceIdType.MESH
ANY = pl.BlockSpec(memory_space=pl.ANY)
IN_VMEM = pl.BlockSpec(memory_space=pltpu.VMEM)
MIB = 2**20


def remote(src, dst, sends, recvs, index, to):
    return pltpu.make_async_remote_copy(
        src_ref=src, dst_ref=dst, send_sem=sends.at[index], recv_sem=recvs.at[index],
        device_id=to, device_id_type=MESH)


class Place:
    def __init__(self, seq_count, wt_count):
        self.nx = 1 << ((seq_count.bit_length() - 1) // 2)
        self.nz = seq_count // self.nx
        self.nc = 2
        self.ny = wt_count // self.nc
        self.seq = lax.axis_index("seq")
        self.wt = lax.axis_index("wt")
        self.z = self.seq // self.nx
        self.x = lax.rem(self.seq, self.nx)
        self.y = self.wt // self.nc
        self.c = lax.rem(self.wt, self.nc)

    def z_at(self, d):
        return lax.rem(self.z + d + self.nz, self.nz)

    def x_at(self, d):
        return lax.rem(self.x + d + self.nx, self.nx)

    def y_at(self, d):
        return lax.rem(self.y + d + self.ny, self.ny)

    def to_z(self, d):
        return (self.z_at(d) * self.nx + self.x, self.wt)

    def to_x(self, d):
        return (self.z * self.nx + self.x_at(d), self.wt)

    def to_y(self, d):
        return (self.seq, self.y_at(d) * self.nc + self.c)

    def to_core(self):
        return (self.seq, self.y * self.nc + 1 - self.c)

    def to_seq(self, d):
        return (lax.rem(self.seq + d, self.nz * self.nx), self.wt)


def meet(peers):
    barrier = pltpu.get_barrier_semaphore()
    for to in peers:
        pl.semaphore_signal(barrier, inc=1, device_id=to, device_id_type=MESH)
    pl.semaphore_wait(barrier, len(peers))


def take_turns(tasks):
    tasks = list(tasks)
    while tasks:
        for task in list(tasks):
            try:
                next(task)
            except StopIteration:
                tasks.remove(task)


def gather_plane(at, own, full, parts, sems):
    zs, zr, xs, xr = sems
    copies = []

    def over_x(k, d, h):
        slot = at.z_at(-k) * at.nx + at.x_at(-d)
        return remote(full.at[slot, h], full.at[slot, h], xs, xr, (k, d - 1, h), at.to_x(d))

    for k in range(at.nz):
        slot = at.z_at(-k) * at.nx + at.x
        for h in range(parts):
            if k:
                remote(full.at[slot, h], full.at[slot, h], zs, zr, (k - 1, h), at.to_z(1)).wait_recv()
            src = full.at[slot, h] if k else own.at[h]
            if k < at.nz - 1:
                copy = remote(src, full.at[slot, h], zs, zr, (k, h), at.to_z(1))
                copy.start()
                copies.append(copy)
            for d in range(1, at.nx):
                copy = remote(src, full.at[slot, h], xs, xr, (k, d - 1, h), at.to_x(d))
                copy.start()
                copies.append(copy)
            yield
    for k in range(at.nz):
        for d in range(1, at.nx):
            for h in range(parts):
                over_x(k, d, h).wait_recv()
                yield
    for copy in copies:
        copy.wait_send()


def gather_plane_sems(at_nz, at_nx, parts):
    dma = pltpu.SemaphoreType.DMA
    return [dma((at_nz, parts)), dma((at_nz, parts)),
            dma((at_nz, at_nx - 1, parts)), dma((at_nz, at_nx - 1, parts))]


def gather_wt(at, own, block, sems, rest=0):
    ys, yr, cs, cr = sems
    copies = []
    for d in range(1, at.ny):
        copy = remote(own, block(at.wt), ys, yr, (d,), at.to_y(d))
        copy.start()
        copies.append(copy)
    copy = remote(own, block(at.wt), cs, cr, (0,), at.to_core())
    copy.start()
    copies.append(copy)
    for _ in range(1 + rest):
        yield
    for d in range(1, at.ny):
        slot = at.y_at(-d) * at.nc + at.c
        remote(block(slot), block(slot), ys, yr, (d,), at.to_y(d)).wait_recv()
        copy = remote(block(slot), block(slot), cs, cr, (d,), at.to_core())
        copy.start()
        copies.append(copy)
        yield
    for d in range(at.ny):
        slot = at.y_at(-d) * at.nc + 1 - at.c
        remote(block(slot), block(slot), cs, cr, (d,), at.to_core()).wait_recv()
        yield
    for copy in copies:
        copy.wait_send()


def wt_sems(ny):
    return [pltpu.SemaphoreType.DMA((ny,)) for _ in range(4)]


def near(at, z=True, x=True, y=True, c=True):
    peers = []
    if z:
        peers += [at.to_z(1), at.to_z(-1)]
    if x:
        peers += [at.to_x(d) for d in range(1, at.nx)]
    if y:
        peers += [at.to_y(d) for d in range(1, at.ny)]
    if c:
        peers += [at.to_core()]
    return peers


def exchange_plane(at, send, recv, ss, rs, rest=0):
    count = at.nz * at.nx
    copies = []
    for d in range(1, count):
        to = lax.rem(at.seq + d, count)
        copy = remote(send.at[to], recv.at[at.seq], ss, rs, (d,), at.to_seq(d))
        copy.start()
        copies.append(copy)
    for _ in range(1 + rest):
        yield
    for d in range(1, count):
        slot = lax.rem(at.seq - d + count, count)
        remote(recv.at[slot], recv.at[slot], ss, rs, (d,), at.to_seq(d)).wait_recv()
    for copy in copies:
        copy.wait_send()


def turn(tasks):
    for task in list(tasks):
        try:
            next(task)
        except StopIteration:
            tasks.remove(task)


def grads_task(at, grad_part, cbuf, qbuf, ybuf, rbuf, abuf, grads_out, block_sems, move_sems, rest=0, hold=0):
    yield from reduce_block(at, grad_part, cbuf, qbuf, ybuf, rbuf, block_sems, rest)
    yield from exchange_plane(at, rbuf, abuf, *move_sems, rest=hold)
    width = rbuf.shape[-1]
    abuf[at.seq] = rbuf[at.seq]
    for s in range(abuf.shape[0]):
        grads_out[:, s * width:(s + 1) * width] = abuf[s].astype(f32)


def to_wt(at, d):
    count = at.ny * at.nc
    return (at.seq, lax.rem(at.wt + d + count, count))


def turns(tasks, count):
    for _ in range(count):
        turn(tasks)


def front_kernel(seq_count, wt_count, chunk, parts, *refs):
    refs = list(refs)

    def take(n):
        out = refs[:n]
        del refs[:n]
        return out

    own, gain_own, w_own, wo_own, pack_own, rate_own, proj_own, g_own = take(8)
    (n_out, w_out, wo_out, g_full, h_full, gate, pre, stream, act, y_ref, hend, sig, u_ref, kq_ref, projected,
     pack, w_rate, w_proj, inverse, gain) = take(20)
    n_full, w_full, wo_full, sbuf, ys, state, kqs, hbuf, part, psend, precv = take(11)
    hsem, local, gs, gr, ss, sr, s1, r1, s2, r2 = take(10)
    nsems, gsems, wsems = take(4), take(4), [take(4), take(4), take(4)]
    at = Place(seq_count, wt_count)
    rows, model = own.shape
    width = act.shape[1]
    rank = w_rate.shape[0]
    tall = kqs.shape[1]
    packs = 128 // tall
    lanes = gain_own.shape[1]
    owned = pack_own.shape[1]
    owner = at.seq * width // owned
    offset = pl.multiple_of(lax.rem(at.seq * width, owned), 128)
    taps = pack.shape[0] - 4

    pieces = [(pack_own.at[:, pl.ds(offset, width)], pack),
              (rate_own.at[:, pl.ds(offset, width)], w_rate),
              (proj_own.at[pl.ds(offset, width), :], w_proj)]
    halves = [w_own.at[:, pl.ds(pl.multiple_of(h * width * seq_count + at.seq * width, 128), width)] for h in range(2)]
    wo_mine = wo_own.at[pl.ds(pl.multiple_of(at.seq * width, 8), width), :]

    def wo_block(slot):
        return wo_full.at[:, pl.ds(pl.multiple_of(slot * lanes, 128), lanes)]

    mine = [pltpu.make_async_copy(halves[h], w_full.at[h, at.wt], local.at[h]) for h in range(2)]
    mine.append(pltpu.make_async_copy(wo_mine, wo_block(at.wt), local.at[3]))
    mine.append(pltpu.make_async_copy(g_own, g_full.at[at.seq], local.at[2]))
    for copy in mine:
        copy.start()
    gain[at.wt] = gain_own[...]
    sbuf[0:8, :] = jnp.zeros((8, width), f32)
    meet([at.to_seq(d) for d in range(1, seq_count)] + [to_wt(at, d) for d in range(1, wt_count)])

    gains = []
    for d in range(1, wt_count):
        copy = remote(gain.at[at.wt], gain.at[at.wt], gs, gr, (d,), to_wt(at, d))
        copy.start()
        gains.append(copy)
    weights = [gather_wt(at, halves[h], lambda slot, h=h: w_full.at[h, slot], wsems[h]) for h in range(2)]
    outward = [gather_wt(at, wo_mine, wo_block, wsems[2])]
    turn(weights)

    def piece_copy(i, d):
        src, dst = pieces[i]
        return pltpu.make_async_remote_copy(src_ref=src, dst_ref=dst, send_sem=ss.at[i, d], recv_sem=sr.at[i],
                                            device_id=to_wt(at, d), device_id_type=MESH)

    @pl.when(at.wt == owner)
    def _():
        for i in range(3):
            pltpu.make_async_copy(*pieces[i], ss.at[i, 0]).start()
            for d in range(1, wt_count):
                piece_copy(i, d).start()

    for d in range(1, wt_count):
        slot = lax.rem(at.wt - d + wt_count, wt_count)
        remote(gain.at[slot], gain.at[slot], gs, gr, (d,), to_wt(at, d)).wait_recv()

    high = rows // parts
    step = 16
    rowing = gather_plane(at, n_full.at[at.seq], n_full, parts, nsems)
    for h in range(parts):
        for i in range(0, high, step):
            at_rows = pl.ds(h * high + i, step)
            x = own[at_rows, :].astype(f32)
            inv = lax.rsqrt(jnp.mean(x * x, axis=-1, keepdims=True) + EPS)
            inverse[at_rows, :] = jnp.broadcast_to(inv, (step, 128))
            unit = x * inv
            for w in range(wt_count):
                n_full[at.seq, h, i:i + step, w * lanes:(w + 1) * lanes] = (
                    unit[:, w * lanes:(w + 1) * lanes] * gain[w]).astype(b16)
        next(rowing)
    turn(outward)
    for k in range(1, at.nz):
        for h in range(parts):
            next(rowing)
    going = [gather_plane(at, g_own, g_full, parts, gsems)]
    turns(going, parts)
    take_turns(weights)
    for copy in mine:
        copy.wait()

    @pl.when(at.wt == owner)
    def _():
        for i in range(3):
            pltpu.make_async_copy(*pieces[i], ss.at[i, 0]).wait()
            for d in range(1, wt_count):
                piece_copy(i, d).wait_send()

    @pl.when(at.wt != owner)
    def _():
        for i in range(3):
            piece_copy(i, 1).wait_recv()

    def mix(slot):
        block = n_full[slot].reshape(rows, model)
        first = pl.multiple_of(slot * rows, rows)
        for h in range(2):
            out = jnp.dot(block, w_full[h].reshape(model, width), preferred_element_type=f32).astype(b16)
            if h:
                gate[pl.ds(first, rows), :] = out
            else:
                stream[pl.ds(first, rows), :] = out
                sbuf[pl.ds(first + 8, rows), :] = out.astype(f32)

    for k in range(at.nz):
        mix(at.z_at(-k) * at.nx + at.x)
    for k in range(at.nz):
        for d in range(1, at.nx):
            for h in range(parts):
                next(rowing)
            mix(at.z_at(-k) * at.nx + at.x_at(-d))
        if k % 2:
            turn(going)
    for _ in rowing:
        pass
    take_turns(outward)
    saves = [pltpu.make_async_copy(n_full, n_out, local.at[0]), pltpu.make_async_copy(w_full, w_out, local.at[1]),
             pltpu.make_async_copy(wo_full, wo_out, local.at[2])]
    for copy in saves:
        copy.start()

    first_sends = []
    bias = pack[taps:taps + 1, :]
    for d in list(range(1, seq_count)) + [0]:
        block = lax.rem(at.seq + d, seq_count)
        first = pl.multiple_of(block * rows, rows)
        total = bias
        window = sbuf[pl.ds(first, rows + 8), :]
        for j in range(taps):
            total = total + pack[j:j + 1, :] * window[9 - taps + j:9 - taps + j + rows]
        pre[pl.ds(first, rows), :] = total
        out = (total * jax.nn.sigmoid(total)).astype(b16)
        act[pl.ds(first, rows), :] = out.astype(f32)
        both = jnp.dot(out, w_proj[...], preferred_element_type=f32)
        part[d, :rank, :] = both[:, :rank]
        narrow = jnp.concatenate([both[:, rank:], jnp.zeros((rows, 128 - tall), f32)], axis=1)
        height = rows // packs
        packed = narrow[:height]
        for i in range(1, packs):
            packed = packed + pltpu.roll(narrow[i * height:(i + 1) * height], i * tall, axis=1)
        part[d, rank:, :] = packed
        if d:
            psend[d] = part[d].astype(b16)
            copy = remote(psend.at[d], precv.at[d], s1, r1, (d,), at.to_seq(d))
            copy.start()
            first_sends.append(copy)
    turns(going, parts)
    total = part[0]
    for d in range(1, seq_count):
        remote(precv.at[d], precv.at[d], s1, r1, (d,), at.to_seq(d)).wait_recv()
        total = total + precv[d].astype(f32)
    projected[at.seq] = total.astype(b16)
    second_sends = []
    for d in range(1, seq_count):
        copy = remote(projected.at[at.seq], projected.at[at.seq], s2, r2, (d,), at.to_seq(d))
        copy.start()
        second_sends.append(copy)
    turns(going, parts)
    for d in range(1, seq_count):
        slot = lax.rem(at.seq - d + seq_count, seq_count)
        remote(projected.at[slot], projected.at[slot], s2, r2, (d,), at.to_seq(d)).wait_recv()

    lane = lax.broadcasted_iota(jnp.int32, (rows, 128), 1)

    def prepare(i):
        first = pl.multiple_of(i * rows, rows)
        here = pl.ds(first, rows)
        packed = projected[i, rank:, :].astype(f32)
        kq = jnp.concatenate([packed] + [pltpu.roll(packed, 128 - j * tall, axis=1) for j in range(1, packs)], axis=0)
        kq_ref[here, :] = kq
        keys = jnp.where(lane < tall // 2, kq, 0.0)
        knorm = jnp.sum(keys * keys, axis=1, keepdims=True)
        s = jax.nn.sigmoid(jnp.dot(projected[i, :rank, :], w_rate[...], preferred_element_type=f32)
                           + pack[taps + 1:taps + 2, :])
        sig[here, :] = s
        rates = s.astype(b16).astype(f32)
        u_ref[here, :] = rates / (1.0 + rates * knorm)

    forward_all(chunk, min(8, seq_count), lambda: turn(going), act, u_ref, kq_ref, ys, h_full, state, kqs, hbuf, hsem,
                prepare)
    y_ref[...] = ys[...].astype(b16)
    hend[...] = state[...]
    take_turns(going)
    for copy in gains + first_sends + second_sends:
        copy.wait_send()
    for copy in saves:
        copy.wait()


def front(tokens, gain, in_weight, out_weight, pack, rate_weight, proj_weight, g_own, states, width, seq_count, wt_count, parts=2):
    rows, model = tokens.shape
    length = rows * seq_count
    rank = rate_weight.shape[0]
    tall = rank + 2 * states * rows // 128
    nx = 1 << ((seq_count.bit_length() - 1) // 2)
    nz = seq_count // nx
    split = (parts, rows // parts, model)
    vmem = pltpu.VMEM
    dma = pltpu.SemaphoreType.DMA

    def like(shape, dtype):
        return jax.ShapeDtypeStruct(shape, dtype)

    weights = (2, wt_count, model // wt_count, width)
    out = pl.pallas_call(
        functools.partial(front_kernel, seq_count, wt_count, rows, parts),
        in_specs=[IN_VMEM] * 2 + [ANY] * 6,
        out_specs=[ANY] * 5 + [IN_VMEM] * 15,
        out_shape=[like((seq_count,) + split, b16), like(weights, b16), like((width, model), b16),
                   like((seq_count,) + split, b16), like((length, states, width), b16),
                   like((length, width), b16), like((length, width), f32), like((length, width), b16),
                   like((length, width), f32), like((length, width), b16), like((states, width), f32),
                   like((length, width), f32), like((length, width), f32), like((length, 128), f32),
                   like((seq_count, tall, 128), b16), like((pack.shape[0], width), f32), like((rank, width), b16),
                   like((width, rank + 2 * states), b16), like((rows, 128), f32),
                   like((wt_count, 1, model // wt_count), f32)],
        scratch_shapes=[vmem((seq_count,) + split, b16), vmem(weights, b16), vmem((width, model), b16), vmem((8 + length, width), f32),
                        vmem((length, width), f32), vmem((states, width), f32), vmem((rows, 2 * states, 128), f32),
                        vmem((2, rows, states, width), b16), vmem((seq_count, tall, 128), f32),
                        vmem((seq_count, tall, 128), b16), vmem((seq_count, tall, 128), b16),
                        dma((2,)), dma((4,)), dma((wt_count,)), dma((wt_count,)), dma((3, wt_count)), dma((3,)),
                        dma((seq_count,)), dma((seq_count,)), dma((seq_count,)), dma((seq_count,))]
        + gather_plane_sems(nz, nx, parts) * 2 + wt_sems(wt_count // 2) * 3,
        compiler_params=pltpu.CompilerParams(collective_id=0, has_side_effects=True, vmem_limit_bytes=58 * MIB),
        name="front",
    )(tokens, gain, in_weight, out_weight, pack, rate_weight, proj_weight, g_own.reshape(split))
    return out


def add_rows(count, store, *terms):
    @pl.loop(0, count)
    def _(i):
        total = terms[0](i).astype(f32)
        for term in terms[1:]:
            total = total + term(i).astype(f32)
        store(i, total)


def reduce_block(at, part, cbuf, qbuf, ybuf, rbuf, sems, rest=0):
    cs, cr, ys, yr = sems
    count = part.shape[0]
    copies = []
    for d in range(at.ny):
        yd = at.y_at(d + 1)
        copy = remote(part.at[:, yd * at.nc + 1 - at.c], cbuf.at[d], cs, cr, (d,), at.to_core())
        copy.start()
        copies.append(copy)
    yield
    for d in range(at.ny):
        mine = at.y_at(d + 1) * at.nc + at.c
        remote(cbuf.at[d], cbuf.at[d], cs, cr, (d,), at.to_core()).wait_recv()
        if d < at.ny - 1:
            def store(i, total):
                qbuf[d, i] = total.astype(qbuf.dtype)
            add_rows(count, store, lambda i: part[i, mine], lambda i: cbuf[d, i])
            copy = remote(qbuf.at[d], ybuf.at[d], ys, yr, (d,), at.to_y(d + 1))
            copy.start()
            copies.append(copy)
            yield
    for _ in range(rest):
        yield
    for d in range(at.ny - 1):
        remote(ybuf.at[d], ybuf.at[d], ys, yr, (d,), at.to_y(d + 1)).wait_recv()

    def keep(i, total):
        rbuf[i] = total.astype(rbuf.dtype)
    add_rows(count, keep, lambda i: part[i, at.wt], lambda i: cbuf[at.ny - 1, i],
             *[lambda i, d=d: ybuf[d, i] for d in range(at.ny - 1)])
    for copy in copies:
        copy.wait_send()


def all_sum(at, box, wbox, sbox, sems):
    s1, r1, s2, r2 = sems
    copies = []
    others = [at.to_core()]
    for d in range(1, at.ny):
        others += [at.to_y(d), (at.seq, at.y_at(d) * at.nc + 1 - at.c)]
    for i, to in enumerate(others):
        copy = remote(box, wbox.at[i], s1, r1, (i,), to)
        copy.start()
        copies.append(copy)
    yield
    for i, copy in enumerate(copies):
        copy.wait()
    total = box[...]
    for i in range(len(others)):
        total = total + wbox[i]
    box[...] = total
    second = []
    count = at.nz * at.nx
    for d in range(1, count):
        copy = remote(box, sbox.at[d], s2, r2, (d,), at.to_seq(d))
        copy.start()
        second.append(copy)
    yield
    for copy in second:
        copy.wait()
    for d in range(1, count):
        total = total + sbox[d]
    box[...] = total


NT = (((1,), (1,)), ((), ()))
TN = (((0,), (0,)), ((), ()))


def dot_of(left, right, dims):
    return lax.dot_general(left, right, dims, preferred_element_type=f32)


def send(src, dst, send_sem, recv_sem, to):
    return pltpu.make_async_remote_copy(src_ref=src, dst_ref=dst, send_sem=send_sem, recv_sem=recv_sem,
                                        device_id=to, device_id_type=MESH)


def pack_rows(wide, narrow, tall):
    packs = 128 // tall
    height = narrow.shape[0] // packs
    packed = narrow[:height]
    for i in range(1, packs):
        packed = packed + pltpu.roll(narrow[i * height:(i + 1) * height], i * tall, axis=1)
    return jnp.concatenate([wide, packed], axis=0)


def unpack_rows(both, rows, tall):
    packed = both[rows:]
    return both[:rows], jnp.concatenate(
        [packed] + [pltpu.roll(packed, 128 - j * tall, axis=1) for j in range(1, 128 // tall)], axis=0)


def back_kernel(seq_count, wt_count, *refs):
    refs = list(refs)

    def take(n):
        out = refs[:n]
        del refs[:n]
        return out

    (a_in, u_in, gs_in, sig_in, pre_in, stream_in, gate_in, normed_in, h_in, wo_in, gated_in,
     w_hbm, kq_in, rate_in, last, early_in, early_hid, w_rate, w_proj, pack, own, g_own, inverse, gain,
     valid) = take(25)
    early = (early_in, early_hid)
    tokens_out, in_out, out_out, rate_out, proj_out, taps_out, bias_out, rbias_out, skip_out, result_out, gain_out = take(11)
    adjoint, after, kqs, hbuf, sums, ga, gu, ebuf, four, three, nbuf, held, held16, window, accs = take(15)
    psend, precv, pown, proj = take(4)
    pbuf, xbuf, zbuf, acc, acc_rate, acc_proj, late, small = take(8)
    small_out, gx, total, wbuf, mypart, bbuf, box, wbox, sbox, w_in, branch = take(11)
    grad_bufs = [take(5) for _ in range(3)]
    small_bufs = take(3)
    hsem, fsem, tsem, nsem, wsem, local, s1, r1, s2, r2, xs, xr, zs, zr, bs, br = take(16)
    gsems, gwsems = take(2), take(4)
    grad_sems = [take(6) for _ in range(3)]
    small_sems, sum_sems = take(4), take(4)

    at = Place(seq_count, wt_count)
    rows, model = own.shape
    width = u_in.shape[1]
    rank = w_rate.shape[0]
    states = adjoint.shape[0]
    tall = 2 * states
    half = hbuf.shape[1]
    slots = pbuf.shape[0]
    pieces = xs.shape[1]
    short = rows // pieces
    taps = pack.shape[0] - 4
    lanes = model // wt_count
    everyone = ([at.to_seq(d) for d in range(1, seq_count)] + [to_wt(at, d) for d in range(1, wt_count)])

    def load_four(b):
        slot = lax.rem(b, 2)
        return [pltpu.make_async_copy(src.at[pl.ds(b * rows, rows)], four.at[slot, i], fsem.at[slot, i])
                for i, src in enumerate((a_in, u_in, gs_in, sig_in))]

    def load_three(b):
        slot = lax.rem(b, 2)
        return ([pltpu.make_async_copy(pre_in.at[pl.ds(b * rows, rows)], window.at[slot], tsem.at[slot, 0])]
                + [pltpu.make_async_copy(src.at[pl.ds(b * rows, rows)], three.at[slot, i], tsem.at[slot, i + 1])
                   for i, src in enumerate((stream_in, gate_in))]
                + [pltpu.make_async_copy(normed_in.at[pl.ds(b * rows, rows)], nbuf.at[slot], nsem.at[slot])])

    def load_h(b, upper):
        return pltpu.make_async_copy(h_in.at[pl.ds(b * rows + upper * half, half)], hbuf.at[1 - upper],
                                     hsem.at[1 - upper])

    def start(copies):
        for copy in copies:
            copy.start()

    def wait(copies):
        for copy in copies:
            copy.wait()

    start(load_four(seq_count - 1))
    start(load_three(seq_count - 1))
    load_h(seq_count - 1, 1).start()
    mine = pltpu.make_async_copy(gated_in.at[at.seq], gx.at[at.wt, at.seq], local.at[0])
    mine.start()
    weights = pltpu.make_async_copy(w_hbm, w_in, local.at[1])
    weights.start()
    adjoint[...] = jnp.zeros_like(adjoint)
    after[...] = last[...]
    accs[...] = jnp.zeros_like(accs)
    box[...] = jnp.zeros_like(box)
    acc_rate[...] = jnp.zeros_like(acc_rate)
    acc_proj[...] = jnp.zeros_like(acc_proj)
    ahead = window.at[2]
    ahead[0:8, :] = jnp.zeros((8, width), f32)

    @pl.loop(0, model // 128)
    def _(i):
        acc[pl.ds(pl.multiple_of(i * 128, 128), 128), :] = jnp.zeros((128, width), f32)

    meet(everyone)

    def fetch(s):
        return pltpu.make_async_copy(wo_in.at[pl.ds(s * width, width)], wbuf.at[s % 2], wsem.at[s % 2])

    def product():
        yield from exchange_plane(at, gated_in, gx.at[at.wt], *gsems, rest=2)
        mine.wait()
        fetch(0).start()
        yield from gather_wt(at, gx.at[at.wt], lambda slot: gx.at[slot], gwsems, rest=2)
        for s in range(seq_count):
            if s + 1 < seq_count:
                fetch(s + 1).start()
            fetch(s).wait()
            term = jnp.dot(gx[:, s].reshape(wt_count * rows, width), wbuf[s % 2], preferred_element_type=f32)
            term = term.reshape(wt_count, rows, lanes)
            if s:
                total[...] += term
            else:
                total[...] = term
        for w in range(wt_count):
            branch[w] = total[w].astype(b16)
        copies = []
        for d in range(1, wt_count):
            to = lax.rem(at.wt + d, wt_count)
            copy = send(branch.at[to], bbuf.at[at.wt], bs.at[d], br.at[d], to_wt(at, d))
            copy.start()
            copies.append(copy)
        bbuf[at.wt] = branch[at.wt]
        for _ in range(10):
            yield
        for d in range(1, wt_count):
            slot = lax.rem(at.wt - d + wt_count, wt_count)
            send(bbuf.at[slot], bbuf.at[slot], bs.at[d], br.at[d], to_wt(at, d)).wait_recv()
        for w in range(wt_count):
            cols = slice(w * lanes, (w + 1) * lanes)
            result_out[:, cols] = ((own[:, cols].astype(f32) + bbuf[w].astype(f32)) * valid[...]).astype(b16)
        for copy in copies:
            copy.wait_send()

    wide = in_out.shape[1] // 2
    stream_out = in_out.at[:, :wide]
    early_out = (in_out.at[:, wide:], out_out)
    tasks = [product()]
    late_tasks = []
    for j in range(2):
        tasks.append(grads_task(at, early[j], *grad_bufs[j], early_out[j], grad_sems[j][:4], grad_sems[j][4:],
                                rest=1, hold=20))
    turn(tasks)

    lane = lax.broadcasted_iota(jnp.int32, (rows, 128), 1)

    def to_owner(b):
        return send(psend.at[b], precv.at[at.seq], s1.at[b], r1.at[at.seq], (b, at.wt))

    def from_other(b):
        return send(precv.at[b], precv.at[b], s1.at[b], r1.at[b], (b, at.wt))

    def to_all(d):
        return send(proj.at[at.seq], proj.at[at.seq], s2.at[d], r2.at[at.seq], at.to_seq(d))

    def from_owner(b):
        return send(proj.at[b], proj.at[b], s2.at[0], r2.at[b], (b, at.wt))

    def adjoint_block(b):
        slot = lax.rem(b, 2)

        @pl.when(b > 0)
        def _():
            start(load_four(b - 1))
        wait(load_four(b))
        a, u, gs, sig = (four.at[slot, i] for i in range(4))
        for upper in (1, 0):
            spread_rows(kq_in, pl.multiple_of(b * rows + upper * half, half), kqs)
            if upper:
                load_h(b, 0).start()
            else:
                @pl.when(b > 0)
                def _():
                    load_h(b - 1, 1).start()
            load_h(b, upper).wait()
            backward_rows(upper * half, adjoint, after, a, u, gs, kqs, hbuf.at[1 - upper], ga, gu, sums)
            ebuf[:, upper * half:(upper + 1) * half] = gather_columns(sums)
        keys = jnp.where(lane < states, kq_in[pl.ds(pl.multiple_of(b * rows, rows), rows), :], 0.0)
        knorm = jnp.sum(keys * keys, axis=1, keepdims=True)
        s = sig[...]
        den = 1.0 + s.astype(b16).astype(f32) * knorm
        g_u = gu[...]
        g_pre = g_u / (den * den) * s * (1.0 - s)
        u_all = u[...]
        g_knorm = -jnp.sum(g_u * u_all * u_all, axis=1, keepdims=True)
        accs[taps + 1:taps + 2, :] += jnp.sum(g_pre, axis=0, keepdims=True)
        accs[taps + 2:taps + 3, :] += jnp.sum(gs[...] * a[...], axis=0, keepdims=True)
        g16 = g_pre.astype(b16)
        acc_rate[...] += dot_of(rate_in[b], g16, TN)
        sums_t = jnp.transpose(jnp.concatenate([ebuf[...], jnp.zeros((128 - tall, rows), f32)], axis=0))
        payload = pack_rows(dot_of(g16, w_rate[...], NT), sums_t + 2.0 * keys * g_knorm, tall)
        held[lax.rem(b, 3)] = ga[...] + gs[...] * pack[taps + 2:taps + 3, :]
        held16[lax.rem(b, 3)] = a[...].astype(b16)

        @pl.when(b != at.seq)
        def _():
            psend[b] = payload.astype(b16)
            to_owner(b).start()

        @pl.when(b == at.seq)
        def _():
            pown[...] = payload

    def sum_block(b):
        @pl.when(b == at.seq)
        def _():
            for d in range(1, seq_count):
                other = lax.rem(at.seq + d, seq_count)
                from_other(other).wait_recv()
                pown[...] += precv[other].astype(f32)
            proj[at.seq] = pown[...].astype(b16)
            for d in range(1, seq_count):
                to_all(d).start()

    def kept(b):
        return lax.rem(b, slots) if slots < seq_count else b

    def piece(p):
        return pl.ds(p * short, short)

    def to_column(b, p):
        zb, xb = b // at.nx, lax.rem(b, at.nx)
        place = lax.rem(at.x - xb + at.nx, at.nx) - 1
        return send(pbuf.at[kept(b), piece(p)], xbuf.at[zb, place, piece(p)], xs.at[kept(b), p],
                    xr.at[zb, place, p], (at.z * at.nx + xb, at.wt))

    def onward(b, p, down):
        zb = b // at.nx
        z = at.z - 1 if down else at.z + 1
        slot = jnp.where(z == zb, at.nz, zb) if down else zb
        return send(pbuf.at[kept(b), piece(p)], zbuf.at[slot, piece(p)], zs.at[kept(b), p], zr.at[slot, p],
                    (z * at.nx + at.x, at.wt))

    def wait_sent(b):
        zb, xb = b // at.nx, lax.rem(b, at.nx)

        @pl.when(at.x != xb)
        def _():
            for p in range(pieces):
                to_column(b, p).wait_send()

        @pl.when((at.x == xb) & (zb > at.z))
        def _():
            for p in range(pieces):
                onward(b, p, False).wait_send()

        @pl.when((at.x == xb) & (zb < at.z))
        def _():
            for p in range(pieces):
                onward(b, p, True).wait_send()

    def conv_block(b):
        slot = lax.rem(b, 2)

        @pl.when(b > 0)
        def _():
            start(load_three(b - 1))

        @pl.when(b != at.seq)
        def _():
            from_owner(b).wait_recv()
        wait(load_three(b))
        wide, narrow = unpack_rows(proj[b].astype(f32), rows, tall)
        narrow = jnp.where(lane < tall, narrow, 0.0)
        wide16, narrow16 = wide.astype(b16), narrow.astype(b16)
        act16 = held16[lax.rem(b, 3)]
        g_act = (dot_of(wide16, w_proj[:, :rank], NT) + dot_of(narrow16[:, :tall], w_proj[:, rank:], NT)
                 + held[lax.rem(b, 3)])
        turned = jnp.concatenate([jnp.transpose(wide), jnp.transpose(narrow)[:tall]], axis=0).astype(b16)
        acc_proj[...] += jnp.dot(turned, act16, preferred_element_type=f32)
        pre = window[slot]
        s = jax.nn.sigmoid(pre)
        g_pre = g_act * s * (1.0 + pre * (1.0 - s))
        wider = jnp.concatenate([g_pre, ahead[0:8, :]], axis=0)
        ahead[0:8, :] = g_pre[0:8]
        accs[taps:taps + 1, :] += jnp.sum(g_pre, axis=0, keepdims=True)
        stream = three[slot, 0].astype(f32)
        g_stream = 0.0
        for j in range(taps):
            moved = wider[taps - 1 - j:taps - 1 - j + rows]
            g_stream = g_stream + pack[j:j + 1, :] * moved
            accs[j:j + 1, :] += jnp.sum(moved * stream, axis=0, keepdims=True)
        g16 = g_stream.astype(b16)
        g_gate = three[slot, 1]
        @pl.when(b == seq_count - 1)
        def _():
            weights.wait()
        if slots < seq_count:
            @pl.when(b + slots < seq_count)
            def _():
                wait_sent(b + slots)
        for m in range(0, model, lanes):
            cols = slice(m, m + lanes)
            g_normed = dot_of(g16, w_in[0, cols, :], NT) + dot_of(g_gate, w_in[1, cols, :], NT)
            box[:, cols] += jnp.sum(g_normed * nbuf[slot, :, cols].astype(f32), axis=0, keepdims=True)
            pbuf[kept(b), :, cols] = g_normed.astype(b16)

        @pl.when(b == at.seq)
        def _():
            mypart[...] = pbuf[kept(b)]

        @pl.when(at.x != lax.rem(b, at.nx))
        def _():
            for p in range(pieces):
                to_column(b, p).start()
        for m in range(0, model, 256):
            acc[m:m + 256, :] += dot_of(nbuf[slot, :, m:m + 256], g16, TN)

    def from_column(b, place, p):
        zb = b // at.nx
        return send(xbuf.at[zb, place, piece(p)], xbuf.at[zb, place, piece(p)], xs.at[0, p], xr.at[zb, place, p],
                    (at.seq, at.wt))

    def arrived(slot, p):
        return send(zbuf.at[slot, piece(p)], zbuf.at[slot, piece(p)], zs.at[0, p], zr.at[slot, p], (at.seq, at.wt))

    step = 16

    def add_column(b, p, base, store, sources):
        zb = b // at.nx
        for place in range(at.nx - 1):
            from_column(b, place, p).wait_recv()
        for slot, there in sources:
            @pl.when(there)
            def _():
                arrived(slot, p).wait_recv()
        for i in range(0, short, step):
            here = pl.ds(p * short + i, step)
            value = base(here).astype(f32)
            for place in range(at.nx - 1):
                value = value + xbuf[zb, place, here, :].astype(f32)
            for slot, there in sources:
                value = value + jnp.where(there, zbuf[slot, here, :].astype(f32), 0.0)
            store(here, value)

    def pass_block(b, hops):
        zb, xb = b // at.nx, lax.rem(b, at.nx)

        @pl.when((at.x == xb) & (((zb > at.z) & (at.z == hops)) | ((zb < at.z) & (at.nz - 1 - at.z == hops))))
        def _():
            def store(here, value):
                pbuf[kept(b), here, :] = value.astype(b16)
            for p in range(pieces):
                add_column(b, p, lambda here: pbuf[kept(b), here, :], store, [(zb, hops > 0)] if hops else [])

                @pl.when(zb > at.z)
                def _():
                    onward(b, p, False).start()

                @pl.when(zb < at.z)
                def _():
                    onward(b, p, True).start()

    def each(i, _):
        b = seq_count - 1 - i

        @pl.when(b >= 0)
        def _():
            adjoint_block(b)

        @pl.when((b + 1 >= 0) & (b + 1 < seq_count))
        def _():
            sum_block(b + 1)

        @pl.when((b + 2 >= 0) & (b + 2 < seq_count))
        def _():
            conv_block(b + 2)
        for hops in range(at.nz - 1):
            later = b + 3 + 2 * hops

            @pl.when((later >= 0) & (later < seq_count))
            def _():
                pass_block(later, hops)
        return 0

    segments = min(8, seq_count)
    for s in range(segments):
        lax.fori_loop(s * seq_count // segments, (s + 1) * seq_count // segments, each, 0)
        turn(tasks)
    lax.fori_loop(seq_count, seq_count + 2, each, 0)

    @pl.loop(0, seq_count)
    def _(i):
        for w in range(wt_count):
            high = late.shape[2]
            at_row = pl.multiple_of(i * (wt_count * high) + w * high, high)
            late[i, w] = acc[pl.ds(at_row, high), :].astype(b16)

    thin = width // wt_count
    for w in range(wt_count):
        cols = slice(w * thin, (w + 1) * thin)
        small[0, w, :rank] = acc_rate[:, cols]
        small[0, w, rank:rank + rank + tall] = acc_proj[:, cols]
        small[0, w, rank + rank + tall:] = accs[:, cols]
    box[...] = box[...] / gain[...]
    late_tasks.append(grads_task(at, late, *grad_bufs[2], stream_out, grad_sems[2][:4], grad_sems[2][4:], hold=4))
    late_tasks.append(reduce_block(at, small, *small_bufs, small_out, small_sems))
    turn(late_tasks)
    lax.fori_loop(seq_count + 2, seq_count + 3, each, 0)
    turn(late_tasks)
    late_tasks.append(all_sum(at, box, wbox, sbox, sum_sems))
    lax.fori_loop(seq_count + 3, seq_count + 3 + 2 * (at.nz - 2), each, 0)
    turn(late_tasks)
    turn(late_tasks)

    def emit(here, g):
        own_rows = own[here, :].astype(f32)
        inv = inverse[here, :]
        scaled = g * gain[...]
        mean = jnp.mean(scaled * own_rows, axis=-1, keepdims=True)
        tokens_out[here, :] = (g_own[here, :].astype(f32) + inv * scaled
                               - own_rows * (inv * inv * inv) * mean)

    def rest():
        for p in range(pieces):
            add_column(at.seq, p, lambda here: mypart[here, :], emit,
                       [(at.z, at.z > 0), (at.nz, at.z < at.nz - 1)])
            yield

    take_turns([rest()] + tasks + late_tasks)
    gain_out[...] = box[...]
    rate_out[...] = small_out[0, :rank, :]
    proj_out[...] = small_out[0, rank:rank + rank + tall, :]
    done = rank + rank + tall
    taps_out[...] = small_out[0, done:done + taps, :]
    bias_out[...] = small_out[0, done + taps:done + taps + 1, :]
    rbias_out[...] = small_out[0, done + taps + 1:done + taps + 2, :]
    skip_out[...] = small_out[0, done + taps + 2:done + taps + 3, :]

    @pl.loop(0, seq_count)
    def _(b):
        @pl.when(b != at.seq)
        def _():
            to_owner(b).wait_send()

    @pl.loop(0, slots)
    def _(b):
        wait_sent(b)
    for d in range(1, seq_count):
        to_all(d).wait_send()


def back(arrays, kq, rate_in, last, early, w_rate, w_proj, pack, own, g_own, inverse, gain, valid,
         seq_count, wt_count):
    gated = arrays[-2]
    w_in = arrays[-1]
    rows, model = own.shape
    width = gated.shape[-1]
    states = last.shape[0]
    tall = 2 * states
    rank = w_rate.shape[0]
    high = early[0].shape[-2]
    half = rows // 2
    nx = 1 << ((seq_count.bit_length() - 1) // 2)
    nz = seq_count // nx
    ny = wt_count // 2
    taps = pack.shape[0] - 4
    payload = (rank + tall * rows // 128, 128)
    block = (seq_count, high, width)
    lanes = model // wt_count
    small_rows = 2 * rank + tall + 8
    thin = width // wt_count
    small_block = (1, small_rows, width // wt_count)
    y_less = max(ny - 1, 1)
    vmem = pltpu.VMEM
    dma = pltpu.SemaphoreType.DMA

    def like(shape, dtype):
        return jax.ShapeDtypeStruct(shape, dtype)

    block_bufs = [vmem((ny,) + block, b16), vmem((y_less,) + block, b16), vmem((y_less,) + block, b16),
                  vmem(block, b16), vmem(block, b16)]
    small_bufs = [vmem((ny,) + small_block, f32), vmem((y_less,) + small_block, f32), vmem((y_less,) + small_block, f32)]
    return pl.pallas_call(
        functools.partial(back_kernel, seq_count, wt_count),
        in_specs=[ANY] * 12 + [IN_VMEM] * 13,
        out_specs=[IN_VMEM] * 11,
        out_shape=[like((rows, model), f32), like((high, 2 * seq_count * width), f32), like((high, seq_count * width), f32),
                   like((rank, thin), f32), like((rank + tall, thin), f32), like((taps, thin), f32), like((1, thin), f32),
                   like((1, thin), f32), like((1, thin), f32), like((rows, model), b16), like((1, model), f32)],
        scratch_shapes=[vmem((states, width), f32), vmem((states, width), f32), vmem((half, tall, 128), f32),
                        vmem((2, half, states, width), b16), vmem((half, tall, 128), f32),
                        vmem((rows, width), f32), vmem((rows, width), f32), vmem((tall, rows), f32),
                        vmem((2, 4, rows, width), f32), vmem((2, 2, rows, width), b16), vmem((2, rows, model), b16),
                        vmem((3, rows, width), f32), vmem((3, rows, width), b16), vmem((3, rows, width), f32),
                        vmem((8, width), f32),
                        vmem((seq_count,) + payload, b16), vmem((seq_count,) + payload, b16), vmem(payload, f32),
                        vmem((seq_count,) + payload, b16),
                        vmem((min(seq_count, 16), rows, model), b16), vmem((nz, nx - 1, rows, model), b16),
                        vmem((nz + 1, rows, model), b16), vmem((model, width), f32), vmem((rank, width), f32),
                        vmem((rank + tall, width), f32), vmem((seq_count, wt_count, high, width), b16),
                        vmem((1, wt_count) + small_block[1:], f32),
                        vmem(small_block, f32),
                        vmem((wt_count, seq_count, rows, width), b16), vmem((wt_count, rows, lanes), f32),
                        vmem((2, width, lanes), b16), vmem((rows, model), b16), vmem((wt_count, rows, lanes), b16),
                        vmem((1, model), f32), vmem((wt_count - 1, 1, model), f32), vmem((seq_count, 1, model), f32), vmem(w_in.shape, b16), vmem((wt_count, rows, lanes), b16)]
        + block_bufs * 3 + small_bufs
        + [dma((2,)), dma((2, 4)), dma((2, 3)), dma((2,)), dma((2,)), dma((2,))] + [dma((seq_count,))] * 4
        + [dma((min(seq_count, 16), 8)), dma((nz, nx - 1, 8)), dma((min(seq_count, 16), 8)), dma((nz + 1, 8)), dma((wt_count,)), dma((wt_count,))]
        + [dma((seq_count,))] * 2 + [dma((ny,))] * 4
        + ([dma((ny,))] * 4 + [dma((seq_count,))] * 2) * 3
        + [dma((ny,))] * 4 + [dma((wt_count - 1,))] * 2 + [dma((seq_count,))] * 2,
        compiler_params=pltpu.CompilerParams(collective_id=5, has_side_effects=True, vmem_limit_bytes=62 * MIB),
        name="back",
    )(*arrays, kq, rate_in, last, *early, w_rate, w_proj, pack, own, g_own, inverse, gain, valid)


def silu_parts(v):
    s = jax.nn.sigmoid(v)
    return v * s, s * (1.0 + v * (1.0 - s))


def on_device(
    tokens,
    lengths,
    norm_gain,
    in_weight,
    conv_taps,
    conv_bias,
    proj_weight,
    rate_weight,
    rate_bias,
    skip_gain,
    out_weight,
    cotangent,
):
    num_seqs, piece_len, model_width = tokens.shape
    inner_width = out_weight.shape[0]
    rate_rank = rate_weight.shape[0]
    states = (proj_weight.shape[1] - rate_rank) // 2
    conv_len = conv_taps.shape[0]
    seq_count = lax.axis_size("seq")
    wt_count = lax.axis_size("wt")
    length = piece_len * seq_count
    rows = num_seqs * length
    own_rows = num_seqs * piece_len
    width = inner_width // seq_count
    place = lax.axis_index("seq")

    own = tokens.reshape(own_rows, model_width)
    positions = place * piece_len + jnp.arange(piece_len, dtype=jnp.int32)
    valid = (positions[None, :] < lengths[:, None]).astype(f32).reshape(own_rows, 1)
    g_own16 = lax.optimization_barrier((cotangent.reshape(own_rows, model_width).astype(f32) * valid).astype(b16))
    pack = jnp.concatenate(
        [conv_taps] + [v[None] for v in (conv_bias, rate_bias, skip_gain, skip_gain)], 0).astype(f32)
    (normed, w_in, w_out, g_out, held, gate16, pre, stream16, act, scanned16, last, sig, u, key_query, projected,
     pack, w_rate, w_proj, inverse_rms, gain) = front(
        own, norm_gain.astype(f32).reshape(1, -1), in_weight, out_weight, pack, rate_weight, proj_weight, g_own16,
        states, width, seq_count, wt_count)
    normed = normed.reshape(rows, model_width)
    g_out = g_out.reshape(rows, model_width)
    w_in = w_in.reshape(2, model_width, width)
    inverse_rms = inverse_rms[:, :1]
    gain = gain.reshape(1, model_width)
    taps = pack[:conv_len]
    skip = pack[conv_len + 2][None]
    gate = gate16.astype(f32)
    rate_in = projected[:, :rate_rank]

    g_gated = jnp.einsum("td,id->ti", g_out, w_out, preferred_element_type=f32)
    gate_silu, gate_slope = silu_parts(gate)
    g_scanned = g_gated * gate_silu
    mixer = scanned16.astype(f32) + skip * act
    gated16 = (mixer * gate_silu).astype(b16)
    g_gate16 = (g_gated * mixer * gate_slope).astype(b16)
    part_out = jnp.einsum("td,ti->di", g_out, gated16, preferred_element_type=f32).astype(b16)
    part_gate = jnp.einsum("td,tk->dk", normed, g_gate16, preferred_element_type=f32).astype(b16)

    def by_owner(array):
        return array.reshape(array.shape[:-2] + (seq_count, wt_count, -1, width))

    (grad_tokens, inw_own, outw_own, ratew_own, projw_own, taps_own, cbias_own, rbias_own, skip_own, result,
     grad_gain) = back(
        (act, u, g_scanned, sig, pre, stream16, g_gate16, normed, held, out_weight,
         gated16.reshape(seq_count, own_rows, width), w_in),
        key_query, rate_in, last, (by_owner(part_gate), by_owner(part_out)), w_rate, w_proj, pack,
        own, g_own16, inverse_rms, gain, valid, seq_count, wt_count)
    result = result.reshape(tokens.shape)
    outw_own = outw_own.T
    projw_own = projw_own.T
    cbias_own, rbias_own, skip_own = cbias_own[0], rbias_own[0], skip_own[0]
    grad_tokens = grad_tokens.reshape(tokens.shape)
    owner = place * wt_count + lax.axis_index("wt")
    gain_own = lax.dynamic_slice_in_dim(grad_gain[0], owner * inw_own.shape[0], inw_own.shape[0], 0)
    return (
        result,
        grad_tokens,
        gain_own,
        inw_own,
        taps_own,
        cbias_own,
        projw_own,
        ratew_own,
        rbias_own,
        skip_own,
        outw_own,
    )


def solution(mesh):
    in_specs = (
        P("wt", "seq", None),
        P("wt"),
        P("wt"),
        P("wt", None),
        P(None, "wt"),
        P("wt"),
        P("wt", None),
        P(None, "wt"),
        P("wt"),
        P("wt"),
        P(None, "wt"),
        P("wt", "seq", None),
    )
    out_specs = (
        P("wt", "seq", None),
        P("wt", "seq", None),
        P(("seq", "wt")),
        P(("seq", "wt"), None),
        P(None, ("seq", "wt")),
        P(("seq", "wt")),
        P(("seq", "wt"), None),
        P(None, ("seq", "wt")),
        P(("seq", "wt")),
        P(("seq", "wt")),
        P(None, ("seq", "wt")),
    )
    return jax.shard_map(
        on_device, mesh=mesh, in_specs=in_specs, out_specs=out_specs, check_vma=False
    )
```

```python
import functools

import jax
import jax.numpy as jnp
from jax import lax
from jax.experimental import pallas as pl
from jax.experimental.pallas import tpu as pltpu
from jax.sharding import PartitionSpec as P

EPS = 1e-05
f32 = jnp.float32
b16 = jnp.bfloat16


def own_lane(tall):
    row = lax.broadcasted_iota(jnp.int32, (tall, 128), 0)
    lane = lax.broadcasted_iota(jnp.int32, (tall, 128), 1)
    return (row == lane).astype(f32)


def spread_rows(kq_ref, first, wide):
    rows, tall, _ = wide.shape
    pick = own_lane(tall)
    picked = [(kq_ref[pl.ds(first + j, 1), :] * pick).astype(b16) for j in range(rows)]
    out = jnp.dot(jnp.concatenate(picked, 0), jnp.ones((128, 128), b16), preferred_element_type=f32)
    wide[...] = out.reshape(rows, tall, 128)


def gather_columns(sums):
    rows, tall, _ = sums.shape
    lane = lax.broadcasted_iota(jnp.int32, (tall, rows), 1)
    out = jnp.zeros((tall, rows), f32)
    for j in range(rows):
        out = jnp.where(lane == j, jnp.sum(sums[j], axis=1, keepdims=True), out)
    return out


def forward_rows(first, state, a_ref, u_ref, kqs, ys, h_ref, step=8):
    chunk, states, width = h_ref.shape
    groups = width // 128

    def body(i, h):
        base = pl.multiple_of(i * step, step)
        for j in range(step):
            t = base + j
            k = jnp.tile(kqs[t, :states], (1, groups))
            q = jnp.tile(kqs[t, states:], (1, groups))
            a = a_ref[pl.ds(first + t, 1), :]
            u = u_ref[pl.ds(first + t, 1), :]
            h_ref[t] = h.astype(b16)
            uk = u * k
            h = (1.0 - uk * k) * h + uk * a
            ys[pl.ds(first + t, 1), :] = jnp.sum(h * q, axis=0, keepdims=True)
        return h

    state[...] = lax.fori_loop(0, chunk // step, body, state[...])


def backward_rows(first, adjoint, after, a_ref, u_ref, g_ref, kqs, h_ref, ga_ref, gu_ref, sums, step=8):
    chunk, states, width = h_ref.shape
    groups = width // 128

    def fold(v):
        out = v[:, :128]
        for i in range(1, groups):
            out = out + v[:, i * 128:(i + 1) * 128]
        return out

    def body(i, carried):
        g, h_after = carried
        base = pl.multiple_of(chunk - step - i * step, step)
        for j in reversed(range(step)):
            t = base + j
            k = jnp.tile(kqs[t, :states], (1, groups))
            q = jnp.tile(kqs[t, states:], (1, groups))
            row = pl.ds(first + t, 1)
            a = a_ref[row, :]
            u = u_ref[row, :]
            gy = g_ref[row, :]
            h = h_ref[t].astype(f32)
            adj = gy * q + g
            sums[t, states:] = fold(gy * h_after)
            p = adj * k
            w = k * h
            d = a - w
            up = u * p
            sums[t, :states] = fold((u * adj) * (d - w))
            ga_ref[row, :] = jnp.sum(up, axis=0, keepdims=True)
            gu_ref[row, :] = jnp.sum(p * d, axis=0, keepdims=True)
            g = adj - k * up
            h_after = h
        return g, h_after

    g, h_after = lax.fori_loop(0, chunk // step, body, (adjoint[...], after[...]))
    adjoint[...] = g
    after[...] = h_after


def forward_all(chunk, segments, between, a_ref, u_ref, kq_ref, ys, h_full, state, kqs, hbuf, hsem, prepare):
    count = a_ref.shape[0] // chunk
    state[...] = jnp.zeros_like(state)

    def save(i):
        return pltpu.make_async_copy(hbuf.at[lax.rem(i, 2)], h_full.at[pl.ds(i * chunk, chunk)], hsem.at[lax.rem(i, 2)])

    def one(i, _):
        @pl.when(i >= 2)
        def _():
            save(i - 2).wait()
        first = pl.multiple_of(i * chunk, chunk)
        prepare(i)
        spread_rows(kq_ref, first, kqs)
        forward_rows(first, state, a_ref, u_ref, kqs, ys, hbuf.at[lax.rem(i, 2)])
        save(i).start()
        return 0

    for s in range(segments):
        lax.fori_loop(s * count // segments, (s + 1) * count // segments, one, 0)
        between()
    save(count - 2).wait()
    save(count - 1).wait()


MESH = pl.DeviceIdType.MESH
ANY = pl.BlockSpec(memory_space=pl.ANY)
IN_VMEM = pl.BlockSpec(memory_space=pltpu.VMEM)
MIB = 2**20


def remote(src, dst, sends, recvs, index, to):
    return pltpu.make_async_remote_copy(
        src_ref=src, dst_ref=dst, send_sem=sends.at[index], recv_sem=recvs.at[index],
        device_id=to, device_id_type=MESH)


class Place:
    def __init__(self, seq_count, wt_count):
        self.nx = 1 << ((seq_count.bit_length() - 1) // 2)
        self.nz = seq_count // self.nx
        self.nc = 2
        self.ny = wt_count // self.nc
        self.seq = lax.axis_index("seq")
        self.wt = lax.axis_index("wt")
        self.z = self.seq // self.nx
        self.x = lax.rem(self.seq, self.nx)
        self.y = self.wt // self.nc
        self.c = lax.rem(self.wt, self.nc)

    def z_at(self, d):
        return lax.rem(self.z + d + self.nz, self.nz)

    def x_at(self, d):
        return lax.rem(self.x + d + self.nx, self.nx)

    def y_at(self, d):
        return lax.rem(self.y + d + self.ny, self.ny)

    def to_z(self, d):
        return (self.z_at(d) * self.nx + self.x, self.wt)

    def to_x(self, d):
        return (self.z * self.nx + self.x_at(d), self.wt)

    def to_y(self, d):
        return (self.seq, self.y_at(d) * self.nc + self.c)

    def to_core(self):
        return (self.seq, self.y * self.nc + 1 - self.c)

    def to_seq(self, d):
        return (lax.rem(self.seq + d, self.nz * self.nx), self.wt)


def meet(peers):
    barrier = pltpu.get_barrier_semaphore()
    for to in peers:
        pl.semaphore_signal(barrier, inc=1, device_id=to, device_id_type=MESH)
    pl.semaphore_wait(barrier, len(peers))


def take_turns(tasks):
    tasks = list(tasks)
    while tasks:
        for task in list(tasks):
            try:
                next(task)
            except StopIteration:
                tasks.remove(task)


def gather_plane(at, own, full, parts, sems):
    zs, zr, xs, xr = sems
    copies = []

    def over_x(k, d, h):
        slot = at.z_at(-k) * at.nx + at.x_at(-d)
        return remote(full.at[slot, h], full.at[slot, h], xs, xr, (k, d - 1, h), at.to_x(d))

    for k in range(at.nz):
        slot = at.z_at(-k) * at.nx + at.x
        for h in range(parts):
            if k:
                remote(full.at[slot, h], full.at[slot, h], zs, zr, (k - 1, h), at.to_z(1)).wait_recv()
            src = full.at[slot, h] if k else own.at[h]
            if k < at.nz - 1:
                copy = remote(src, full.at[slot, h], zs, zr, (k, h), at.to_z(1))
                copy.start()
                copies.append(copy)
            for d in range(1, at.nx):
                copy = remote(src, full.at[slot, h], xs, xr, (k, d - 1, h), at.to_x(d))
                copy.start()
                copies.append(copy)
            yield
    for k in range(at.nz):
        for d in range(1, at.nx):
            for h in range(parts):
                over_x(k, d, h).wait_recv()
                yield
    for copy in copies:
        copy.wait_send()


def gather_plane_sems(at_nz, at_nx, parts):
    dma = pltpu.SemaphoreType.DMA
    return [dma((at_nz, parts)), dma((at_nz, parts)),
            dma((at_nz, at_nx - 1, parts)), dma((at_nz, at_nx - 1, parts))]


def gather_wt(at, own, block, sems, rest=0):
    ys, yr, cs, cr = sems
    copies = []
    for d in range(1, at.ny):
        copy = remote(own, block(at.wt), ys, yr, (d,), at.to_y(d))
        copy.start()
        copies.append(copy)
    copy = remote(own, block(at.wt), cs, cr, (0,), at.to_core())
    copy.start()
    copies.append(copy)
    for _ in range(1 + rest):
        yield
    for d in range(1, at.ny):
        slot = at.y_at(-d) * at.nc + at.c
        remote(block(slot), block(slot), ys, yr, (d,), at.to_y(d)).wait_recv()
        copy = remote(block(slot), block(slot), cs, cr, (d,), at.to_core())
        copy.start()
        copies.append(copy)
        yield
    for d in range(at.ny):
        slot = at.y_at(-d) * at.nc + 1 - at.c
        remote(block(slot), block(slot), cs, cr, (d,), at.to_core()).wait_recv()
        yield
    for copy in copies:
        copy.wait_send()


def wt_sems(ny):
    return [pltpu.SemaphoreType.DMA((ny,)) for _ in range(4)]


def near(at, z=True, x=True, y=True, c=True):
    peers = []
    if z:
        peers += [at.to_z(1), at.to_z(-1)]
    if x:
        peers += [at.to_x(d) for d in range(1, at.nx)]
    if y:
        peers += [at.to_y(d) for d in range(1, at.ny)]
    if c:
        peers += [at.to_core()]
    return peers


def exchange_plane(at, send, recv, ss, rs, rest=0):
    count = at.nz * at.nx
    copies = []
    for d in range(1, count):
        to = lax.rem(at.seq + d, count)
        copy = remote(send.at[to], recv.at[at.seq], ss, rs, (d,), at.to_seq(d))
        copy.start()
        copies.append(copy)
    for _ in range(1 + rest):
        yield
    for d in range(1, count):
        slot = lax.rem(at.seq - d + count, count)
        remote(recv.at[slot], recv.at[slot], ss, rs, (d,), at.to_seq(d)).wait_recv()
    for copy in copies:
        copy.wait_send()


def turn(tasks):
    for task in list(tasks):
        try:
            next(task)
        except StopIteration:
            tasks.remove(task)


def grads_task(at, grad_part, cbuf, qbuf, ybuf, rbuf, abuf, grads_out, block_sems, move_sems, rest=0, hold=0):
    yield from reduce_block(at, grad_part, cbuf, qbuf, ybuf, rbuf, block_sems, rest)
    yield from exchange_plane(at, rbuf, abuf, *move_sems, rest=hold)
    width = rbuf.shape[-1]
    abuf[at.seq] = rbuf[at.seq]
    for s in range(abuf.shape[0]):
        grads_out[:, s * width:(s + 1) * width] = abuf[s].astype(f32)


def to_wt(at, d):
    count = at.ny * at.nc
    return (at.seq, lax.rem(at.wt + d + count, count))


def turns(tasks, count):
    for _ in range(count):
        turn(tasks)


def front_kernel(seq_count, wt_count, chunk, parts, *refs):
    refs = list(refs)

    def take(n):
        out = refs[:n]
        del refs[:n]
        return out

    own, gain_own, w_own, wo_own, pack_own, rate_own, proj_own, g_own = take(8)
    (n_out, w_out, wo_out, g_full, h_full, gate, pre, stream, act, y_ref, hend, sig, u_ref, kq_ref, projected,
     pack, w_rate, w_proj, inverse, gain) = take(20)
    n_full, w_full, wo_full, sbuf, ys, state, kqs, hbuf, part, psend, precv = take(11)
    hsem, local, gs, gr, ss, sr, s1, r1, s2, r2 = take(10)
    nsems, gsems, wsems = take(4), take(4), [take(4), take(4), take(4)]
    at = Place(seq_count, wt_count)
    rows, model = own.shape
    width = act.shape[1]
    rank = w_rate.shape[0]
    tall = kqs.shape[1]
    packs = 128 // tall
    lanes = gain_own.shape[1]
    owned = pack_own.shape[1]
    owner = at.seq * width // owned
    offset = pl.multiple_of(lax.rem(at.seq * width, owned), 128)
    taps = pack.shape[0] - 4

    pieces = [(pack_own.at[:, pl.ds(offset, width)], pack),
              (rate_own.at[:, pl.ds(offset, width)], w_rate),
              (proj_own.at[pl.ds(offset, width), :], w_proj)]
    halves = [w_own.at[:, pl.ds(pl.multiple_of(h * width * seq_count + at.seq * width, 128), width)] for h in range(2)]
    wo_mine = wo_own.at[pl.ds(pl.multiple_of(at.seq * width, 8), width), :]

    def wo_block(slot):
        return wo_full.at[:, pl.ds(pl.multiple_of(slot * lanes, 128), lanes)]

    mine = [pltpu.make_async_copy(halves[h], w_full.at[h, at.wt], local.at[h]) for h in range(2)]
    mine.append(pltpu.make_async_copy(wo_mine, wo_block(at.wt), local.at[3]))
    mine.append(pltpu.make_async_copy(g_own, g_full.at[at.seq], local.at[2]))
    for copy in mine:
        copy.start()
    gain[at.wt] = gain_own[...]
    sbuf[0:8, :] = jnp.zeros((8, width), f32)
    step = 16
    barrier = pltpu.get_barrier_semaphore()
    peers = [at.to_seq(d) for d in range(1, seq_count)] + [to_wt(at, d) for d in range(1, wt_count)]
    for to in peers:
        pl.semaphore_signal(barrier, inc=1, device_id=to, device_id_type=MESH)
    for i in range(0, rows, step):
        x = own[i:i + step, :].astype(f32)
        inv = lax.rsqrt(jnp.mean(x * x, axis=-1, keepdims=True) + EPS)
        inverse[i:i + step, :] = jnp.broadcast_to(inv, (step, 128))
    pl.semaphore_wait(barrier, len(peers))

    gains = []
    for d in range(1, wt_count):
        copy = remote(gain.at[at.wt], gain.at[at.wt], gs, gr, (d,), to_wt(at, d))
        copy.start()
        gains.append(copy)
    weights = [gather_wt(at, halves[h], lambda slot, h=h: w_full.at[h, slot], wsems[h]) for h in range(2)]
    outward = [gather_wt(at, wo_mine, wo_block, wsems[2])]
    turn(weights)

    def piece_copy(i, d):
        src, dst = pieces[i]
        return pltpu.make_async_remote_copy(src_ref=src, dst_ref=dst, send_sem=ss.at[i, d], recv_sem=sr.at[i],
                                            device_id=to_wt(at, d), device_id_type=MESH)

    @pl.when(at.wt == owner)
    def _():
        for i in range(3):
            pltpu.make_async_copy(*pieces[i], ss.at[i, 0]).start()
            for d in range(1, wt_count):
                piece_copy(i, d).start()

    for d in range(1, wt_count):
        slot = lax.rem(at.wt - d + wt_count, wt_count)
        remote(gain.at[slot], gain.at[slot], gs, gr, (d,), to_wt(at, d)).wait_recv()

    high = rows // parts
    rowing = gather_plane(at, n_full.at[at.seq], n_full, parts, nsems)
    for h in range(parts):
        for i in range(0, high, step):
            at_rows = pl.ds(h * high + i, step)
            x = own[at_rows, :].astype(f32)
            unit = x * inverse[at_rows, :][:, :1]
            for w in range(wt_count):
                n_full[at.seq, h, i:i + step, w * lanes:(w + 1) * lanes] = (
                    unit[:, w * lanes:(w + 1) * lanes] * gain[w]).astype(b16)
        next(rowing)
    turn(outward)
    for k in range(1, at.nz):
        for h in range(parts):
            next(rowing)
    going = [gather_plane(at, g_own, g_full, parts, gsems)]
    turns(going, parts)
    take_turns(weights)
    for copy in mine:
        copy.wait()

    @pl.when(at.wt == owner)
    def _():
        for i in range(3):
            pltpu.make_async_copy(*pieces[i], ss.at[i, 0]).wait()
            for d in range(1, wt_count):
                piece_copy(i, d).wait_send()

    @pl.when(at.wt != owner)
    def _():
        for i in range(3):
            piece_copy(i, 1).wait_recv()

    def mix(slot):
        block = n_full[slot].reshape(rows, model)
        first = pl.multiple_of(slot * rows, rows)
        for h in range(2):
            out = jnp.dot(block, w_full[h].reshape(model, width), preferred_element_type=f32).astype(b16)
            if h:
                gate[pl.ds(first, rows), :] = out
            else:
                stream[pl.ds(first, rows), :] = out
                sbuf[pl.ds(first + 8, rows), :] = out.astype(f32)

    for k in range(at.nz):
        mix(at.z_at(-k) * at.nx + at.x)
    for k in range(at.nz):
        for d in range(1, at.nx):
            for h in range(parts):
                next(rowing)
            mix(at.z_at(-k) * at.nx + at.x_at(-d))
        if k % 2:
            turn(going)
    for _ in rowing:
        pass
    take_turns(outward)
    saves = [pltpu.make_async_copy(n_full, n_out, local.at[0]), pltpu.make_async_copy(w_full, w_out, local.at[1]),
             pltpu.make_async_copy(wo_full, wo_out, local.at[2])]
    for copy in saves:
        copy.start()

    first_sends = []
    bias = pack[taps:taps + 1, :]
    for d in list(range(1, seq_count)) + [0]:
        block = lax.rem(at.seq + d, seq_count)
        first = pl.multiple_of(block * rows, rows)
        total = bias
        window = sbuf[pl.ds(first, rows + 8), :]
        for j in range(taps):
            total = total + pack[j:j + 1, :] * window[9 - taps + j:9 - taps + j + rows]
        pre[pl.ds(first, rows), :] = total
        out = (total * jax.nn.sigmoid(total)).astype(b16)
        act[pl.ds(first, rows), :] = out.astype(f32)
        both = jnp.dot(out, w_proj[...], preferred_element_type=f32)
        part[d, :rank, :] = both[:, :rank]
        narrow = jnp.concatenate([both[:, rank:], jnp.zeros((rows, 128 - tall), f32)], axis=1)
        height = rows // packs
        packed = narrow[:height]
        for i in range(1, packs):
            packed = packed + pltpu.roll(narrow[i * height:(i + 1) * height], i * tall, axis=1)
        part[d, rank:, :] = packed
        if d:
            psend[d] = part[d].astype(b16)
            copy = remote(psend.at[d], precv.at[d], s1, r1, (d,), at.to_seq(d))
            copy.start()
            first_sends.append(copy)
    turns(going, parts)
    total = part[0]
    for d in range(1, seq_count):
        remote(precv.at[d], precv.at[d], s1, r1, (d,), at.to_seq(d)).wait_recv()
        total = total + precv[d].astype(f32)
    projected[at.seq] = total.astype(b16)
    second_sends = []
    for d in range(1, seq_count):
        copy = remote(projected.at[at.seq], projected.at[at.seq], s2, r2, (d,), at.to_seq(d))
        copy.start()
        second_sends.append(copy)
    turns(going, parts)
    for d in range(1, seq_count):
        slot = lax.rem(at.seq - d + seq_count, seq_count)
        remote(projected.at[slot], projected.at[slot], s2, r2, (d,), at.to_seq(d)).wait_recv()

    lane = lax.broadcasted_iota(jnp.int32, (rows, 128), 1)

    def prepare(i):
        first = pl.multiple_of(i * rows, rows)
        here = pl.ds(first, rows)
        packed = projected[i, rank:, :].astype(f32)
        kq = jnp.concatenate([packed] + [pltpu.roll(packed, 128 - j * tall, axis=1) for j in range(1, packs)], axis=0)
        kq_ref[here, :] = kq
        keys = jnp.where(lane < tall // 2, kq, 0.0)
        knorm = jnp.sum(keys * keys, axis=1, keepdims=True)
        s = jax.nn.sigmoid(jnp.dot(projected[i, :rank, :], w_rate[...], preferred_element_type=f32)
                           + pack[taps + 1:taps + 2, :])
        sig[here, :] = s
        rates = s.astype(b16).astype(f32)
        u_ref[here, :] = rates / (1.0 + rates * knorm)

    forward_all(chunk, min(8, seq_count), lambda: turn(going), act, u_ref, kq_ref, ys, h_full, state, kqs, hbuf, hsem,
                prepare)
    y_ref[...] = ys[...].astype(b16)
    hend[...] = state[...]
    take_turns(going)
    for copy in gains + first_sends + second_sends:
        copy.wait_send()
    for copy in saves:
        copy.wait()


def front(tokens, gain, in_weight, out_weight, pack, rate_weight, proj_weight, g_own, states, width, seq_count, wt_count, parts=2):
    rows, model = tokens.shape
    length = rows * seq_count
    rank = rate_weight.shape[0]
    tall = rank + 2 * states * rows // 128
    nx = 1 << ((seq_count.bit_length() - 1) // 2)
    nz = seq_count // nx
    split = (parts, rows // parts, model)
    vmem = pltpu.VMEM
    dma = pltpu.SemaphoreType.DMA

    def like(shape, dtype):
        return jax.ShapeDtypeStruct(shape, dtype)

    weights = (2, wt_count, model // wt_count, width)
    out = pl.pallas_call(
        functools.partial(front_kernel, seq_count, wt_count, rows, parts),
        in_specs=[IN_VMEM] * 2 + [ANY] * 6,
        out_specs=[ANY] * 5 + [IN_VMEM] * 15,
        out_shape=[like((seq_count,) + split, b16), like(weights, b16), like((width, model), b16),
                   like((seq_count,) + split, b16), like((length, states, width), b16),
                   like((length, width), b16), like((length, width), f32), like((length, width), b16),
                   like((length, width), f32), like((length, width), b16), like((states, width), f32),
                   like((length, width), f32), like((length, width), f32), like((length, 128), f32),
                   like((seq_count, tall, 128), b16), like((pack.shape[0], width), f32), like((rank, width), b16),
                   like((width, rank + 2 * states), b16), like((rows, 128), f32),
                   like((wt_count, 1, model // wt_count), f32)],
        scratch_shapes=[vmem((seq_count,) + split, b16), vmem(weights, b16), vmem((width, model), b16), vmem((8 + length, width), f32),
                        vmem((length, width), f32), vmem((states, width), f32), vmem((rows, 2 * states, 128), f32),
                        vmem((2, rows, states, width), b16), vmem((seq_count, tall, 128), f32),
                        vmem((seq_count, tall, 128), b16), vmem((seq_count, tall, 128), b16),
                        dma((2,)), dma((4,)), dma((wt_count,)), dma((wt_count,)), dma((3, wt_count)), dma((3,)),
                        dma((seq_count,)), dma((seq_count,)), dma((seq_count,)), dma((seq_count,))]
        + gather_plane_sems(nz, nx, parts) * 2 + wt_sems(wt_count // 2) * 3,
        compiler_params=pltpu.CompilerParams(collective_id=0, has_side_effects=True, vmem_limit_bytes=58 * MIB),
        name="front",
    )(tokens, gain, in_weight, out_weight, pack, rate_weight, proj_weight, g_own.reshape(split))
    return out


def add_rows(count, store, *terms):
    @pl.loop(0, count)
    def _(i):
        total = terms[0](i).astype(f32)
        for term in terms[1:]:
            total = total + term(i).astype(f32)
        store(i, total)


def reduce_block(at, part, cbuf, qbuf, ybuf, rbuf, sems, rest=0):
    cs, cr, ys, yr = sems
    count = part.shape[0]
    copies = []
    for d in range(at.ny):
        yd = at.y_at(d + 1)
        copy = remote(part.at[:, yd * at.nc + 1 - at.c], cbuf.at[d], cs, cr, (d,), at.to_core())
        copy.start()
        copies.append(copy)
    yield
    for d in range(at.ny):
        mine = at.y_at(d + 1) * at.nc + at.c
        remote(cbuf.at[d], cbuf.at[d], cs, cr, (d,), at.to_core()).wait_recv()
        if d < at.ny - 1:
            def store(i, total):
                qbuf[d, i] = total.astype(qbuf.dtype)
            add_rows(count, store, lambda i: part[i, mine], lambda i: cbuf[d, i])
            copy = remote(qbuf.at[d], ybuf.at[d], ys, yr, (d,), at.to_y(d + 1))
            copy.start()
            copies.append(copy)
            yield
    for _ in range(rest):
        yield
    for d in range(at.ny - 1):
        remote(ybuf.at[d], ybuf.at[d], ys, yr, (d,), at.to_y(d + 1)).wait_recv()

    def keep(i, total):
        rbuf[i] = total.astype(rbuf.dtype)
    add_rows(count, keep, lambda i: part[i, at.wt], lambda i: cbuf[at.ny - 1, i],
             *[lambda i, d=d: ybuf[d, i] for d in range(at.ny - 1)])
    for copy in copies:
        copy.wait_send()


def all_sum(at, box, wbox, sbox, sems):
    s1, r1, s2, r2 = sems
    copies = []
    others = [at.to_core()]
    for d in range(1, at.ny):
        others += [at.to_y(d), (at.seq, at.y_at(d) * at.nc + 1 - at.c)]
    for i, to in enumerate(others):
        copy = remote(box, wbox.at[i], s1, r1, (i,), to)
        copy.start()
        copies.append(copy)
    yield
    for i, copy in enumerate(copies):
        copy.wait()
    total = box[...]
    for i in range(len(others)):
        total = total + wbox[i]
    box[...] = total
    second = []
    count = at.nz * at.nx
    for d in range(1, count):
        copy = remote(box, sbox.at[d], s2, r2, (d,), at.to_seq(d))
        copy.start()
        second.append(copy)
    yield
    for copy in second:
        copy.wait()
    for d in range(1, count):
        total = total + sbox[d]
    box[...] = total


NT = (((1,), (1,)), ((), ()))
TN = (((0,), (0,)), ((), ()))


def dot_of(left, right, dims):
    return lax.dot_general(left, right, dims, preferred_element_type=f32)


def send(src, dst, send_sem, recv_sem, to):
    return pltpu.make_async_remote_copy(src_ref=src, dst_ref=dst, send_sem=send_sem, recv_sem=recv_sem,
                                        device_id=to, device_id_type=MESH)


def pack_rows(wide, narrow, tall):
    packs = 128 // tall
    height = narrow.shape[0] // packs
    packed = narrow[:height]
    for i in range(1, packs):
        packed = packed + pltpu.roll(narrow[i * height:(i + 1) * height], i * tall, axis=1)
    return jnp.concatenate([wide, packed], axis=0)


def unpack_rows(both, rows, tall):
    packed = both[rows:]
    return both[:rows], jnp.concatenate(
        [packed] + [pltpu.roll(packed, 128 - j * tall, axis=1) for j in range(1, 128 // tall)], axis=0)


def back_kernel(seq_count, wt_count, *refs):
    refs = list(refs)

    def take(n):
        out = refs[:n]
        del refs[:n]
        return out

    (a_in, u_in, gs_in, sig_in, pre_in, stream_in, gate_in, normed_in, h_in, wo_in, gated_in,
     w_hbm, kq_in, rate_in, last, early_in, early_hid, w_rate, w_proj, pack, own, g_own, inverse, gain,
     valid) = take(25)
    early = (early_in, early_hid)
    tokens_out, in_out, out_out, rate_out, proj_out, taps_out, bias_out, rbias_out, skip_out, result_out, gain_out = take(11)
    adjoint, after, kqs, hbuf, sums, ga, gu, ebuf, four, three, nbuf, held, held16, window, accs = take(15)
    psend, precv, pown, proj = take(4)
    pbuf, xbuf, zbuf, acc, acc_rate, acc_proj, late, small = take(8)
    small_out, gx, total, wbuf, mypart, bbuf, box, wbox, sbox, w_in, branch = take(11)
    grad_bufs = [take(5) for _ in range(3)]
    small_bufs = take(3)
    hsem, fsem, tsem, nsem, wsem, local, s1, r1, s2, r2, xs, xr, zs, zr, bs, br = take(16)
    gsems, gwsems = take(2), take(4)
    grad_sems = [take(6) for _ in range(3)]
    small_sems, sum_sems = take(4), take(4)

    at = Place(seq_count, wt_count)
    rows, model = own.shape
    width = u_in.shape[1]
    rank = w_rate.shape[0]
    states = adjoint.shape[0]
    tall = 2 * states
    half = hbuf.shape[1]
    slots = pbuf.shape[0]
    pieces = xs.shape[1]
    short = rows // pieces
    taps = pack.shape[0] - 4
    lanes = model // wt_count
    everyone = ([at.to_seq(d) for d in range(1, seq_count)] + [to_wt(at, d) for d in range(1, wt_count)])

    def load_four(b):
        slot = lax.rem(b, 2)
        return [pltpu.make_async_copy(src.at[pl.ds(b * rows, rows)], four.at[slot, i], fsem.at[slot, i])
                for i, src in enumerate((a_in, u_in, gs_in, sig_in))]

    def load_three(b):
        slot = lax.rem(b, 2)
        return ([pltpu.make_async_copy(pre_in.at[pl.ds(b * rows, rows)], window.at[slot], tsem.at[slot, 0])]
                + [pltpu.make_async_copy(src.at[pl.ds(b * rows, rows)], three.at[slot, i], tsem.at[slot, i + 1])
                   for i, src in enumerate((stream_in, gate_in))]
                + [pltpu.make_async_copy(normed_in.at[pl.ds(b * rows, rows)], nbuf.at[slot], nsem.at[slot])])

    def load_h(b, upper):
        return pltpu.make_async_copy(h_in.at[pl.ds(b * rows + upper * half, half)], hbuf.at[1 - upper],
                                     hsem.at[1 - upper])

    def start(copies):
        for copy in copies:
            copy.start()

    def wait(copies):
        for copy in copies:
            copy.wait()

    start(load_four(seq_count - 1))
    start(load_three(seq_count - 1))
    load_h(seq_count - 1, 1).start()
    mine = pltpu.make_async_copy(gated_in.at[at.seq], gx.at[at.wt, at.seq], local.at[0])
    mine.start()
    weights = pltpu.make_async_copy(w_hbm, w_in, local.at[1])
    weights.start()
    adjoint[...] = jnp.zeros_like(adjoint)
    after[...] = last[...]
    accs[...] = jnp.zeros_like(accs)
    box[...] = jnp.zeros_like(box)
    acc_rate[...] = jnp.zeros_like(acc_rate)
    acc_proj[...] = jnp.zeros_like(acc_proj)
    ahead = window.at[2]
    ahead[0:8, :] = jnp.zeros((8, width), f32)

    @pl.loop(0, model // 128)
    def _(i):
        acc[pl.ds(pl.multiple_of(i * 128, 128), 128), :] = jnp.zeros((128, width), f32)

    meet(everyone)

    def fetch(s):
        return pltpu.make_async_copy(wo_in.at[pl.ds(s * width, width)], wbuf.at[s % 2], wsem.at[s % 2])

    def product():
        yield from exchange_plane(at, gated_in, gx.at[at.wt], *gsems, rest=2)
        mine.wait()
        fetch(0).start()
        yield from gather_wt(at, gx.at[at.wt], lambda slot: gx.at[slot], gwsems, rest=2)
        for s in range(seq_count):
            if s + 1 < seq_count:
                fetch(s + 1).start()
            fetch(s).wait()
            term = jnp.dot(gx[:, s].reshape(wt_count * rows, width), wbuf[s % 2], preferred_element_type=f32)
            term = term.reshape(wt_count, rows, lanes)
            if s:
                total[...] += term
            else:
                total[...] = term
        for w in range(wt_count):
            branch[w] = total[w].astype(b16)
        copies = []
        for d in range(1, wt_count):
            to = lax.rem(at.wt + d, wt_count)
            copy = send(branch.at[to], bbuf.at[at.wt], bs.at[d], br.at[d], to_wt(at, d))
            copy.start()
            copies.append(copy)
        bbuf[at.wt] = branch[at.wt]
        for _ in range(10):
            yield
        for d in range(1, wt_count):
            slot = lax.rem(at.wt - d + wt_count, wt_count)
            send(bbuf.at[slot], bbuf.at[slot], bs.at[d], br.at[d], to_wt(at, d)).wait_recv()
        for w in range(wt_count):
            cols = slice(w * lanes, (w + 1) * lanes)
            result_out[:, cols] = ((own[:, cols].astype(f32) + bbuf[w].astype(f32)) * valid[...]).astype(b16)
        for copy in copies:
            copy.wait_send()

    wide = in_out.shape[1] // 2
    stream_out = in_out.at[:, :wide]
    early_out = (in_out.at[:, wide:], out_out)
    tasks = [product()]
    late_tasks = []
    for j in range(2):
        tasks.append(grads_task(at, early[j], *grad_bufs[j], early_out[j], grad_sems[j][:4], grad_sems[j][4:],
                                rest=1, hold=20))
    turn(tasks)

    lane = lax.broadcasted_iota(jnp.int32, (rows, 128), 1)

    def to_owner(b):
        return send(psend.at[b], precv.at[at.seq], s1.at[b], r1.at[at.seq], (b, at.wt))

    def from_other(b):
        return send(precv.at[b], precv.at[b], s1.at[b], r1.at[b], (b, at.wt))

    def to_all(d):
        return send(proj.at[at.seq], proj.at[at.seq], s2.at[d], r2.at[at.seq], at.to_seq(d))

    def from_owner(b):
        return send(proj.at[b], proj.at[b], s2.at[0], r2.at[b], (b, at.wt))

    def adjoint_block(b):
        slot = lax.rem(b, 2)

        @pl.when(b > 0)
        def _():
            start(load_four(b - 1))
        wait(load_four(b))
        a, u, gs, sig = (four.at[slot, i] for i in range(4))
        for upper in (1, 0):
            spread_rows(kq_in, pl.multiple_of(b * rows + upper * half, half), kqs)
            if upper:
                load_h(b, 0).start()
            else:
                @pl.when(b > 0)
                def _():
                    load_h(b - 1, 1).start()
            load_h(b, upper).wait()
            backward_rows(upper * half, adjoint, after, a, u, gs, kqs, hbuf.at[1 - upper], ga, gu, sums)
            ebuf[:, upper * half:(upper + 1) * half] = gather_columns(sums)
        keys = jnp.where(lane < states, kq_in[pl.ds(pl.multiple_of(b * rows, rows), rows), :], 0.0)
        knorm = jnp.sum(keys * keys, axis=1, keepdims=True)
        s = sig[...]
        den = 1.0 + s.astype(b16).astype(f32) * knorm
        g_u = gu[...]
        g_pre = g_u / (den * den) * s * (1.0 - s)
        u_all = u[...]
        g_knorm = -jnp.sum(g_u * u_all * u_all, axis=1, keepdims=True)
        accs[taps + 1:taps + 2, :] += jnp.sum(g_pre, axis=0, keepdims=True)
        accs[taps + 2:taps + 3, :] += jnp.sum(gs[...] * a[...], axis=0, keepdims=True)
        g16 = g_pre.astype(b16)
        acc_rate[...] += dot_of(rate_in[b], g16, TN)
        sums_t = jnp.transpose(jnp.concatenate([ebuf[...], jnp.zeros((128 - tall, rows), f32)], axis=0))
        payload = pack_rows(dot_of(g16, w_rate[...], NT), sums_t + 2.0 * keys * g_knorm, tall)
        held[lax.rem(b, 3)] = ga[...] + gs[...] * pack[taps + 2:taps + 3, :]
        held16[lax.rem(b, 3)] = a[...].astype(b16)

        @pl.when(b != at.seq)
        def _():
            psend[b] = payload.astype(b16)
            to_owner(b).start()

        @pl.when(b == at.seq)
        def _():
            pown[...] = payload

    def sum_block(b):
        @pl.when(b == at.seq)
        def _():
            for d in range(1, seq_count):
                other = lax.rem(at.seq + d, seq_count)
                from_other(other).wait_recv()
                pown[...] += precv[other].astype(f32)
            proj[at.seq] = pown[...].astype(b16)
            for d in range(1, seq_count):
                to_all(d).start()

    def kept(b):
        return lax.rem(b, slots) if slots < seq_count else b

    def piece(p):
        return pl.ds(p * short, short)

    def to_column(b, p):
        zb, xb = b // at.nx, lax.rem(b, at.nx)
        place = lax.rem(at.x - xb + at.nx, at.nx) - 1
        return send(pbuf.at[kept(b), piece(p)], xbuf.at[zb, place, piece(p)], xs.at[kept(b), p],
                    xr.at[zb, place, p], (at.z * at.nx + xb, at.wt))

    def onward(b, p, down):
        zb = b // at.nx
        z = at.z - 1 if down else at.z + 1
        slot = jnp.where(z == zb, at.nz, zb) if down else zb
        return send(pbuf.at[kept(b), piece(p)], zbuf.at[slot, piece(p)], zs.at[kept(b), p], zr.at[slot, p],
                    (z * at.nx + at.x, at.wt))

    def wait_sent(b):
        zb, xb = b // at.nx, lax.rem(b, at.nx)

        @pl.when(at.x != xb)
        def _():
            for p in range(pieces):
                to_column(b, p).wait_send()

        @pl.when((at.x == xb) & (zb > at.z))
        def _():
            for p in range(pieces):
                onward(b, p, False).wait_send()

        @pl.when((at.x == xb) & (zb < at.z))
        def _():
            for p in range(pieces):
                onward(b, p, True).wait_send()

    def conv_block(b):
        slot = lax.rem(b, 2)

        @pl.when(b > 0)
        def _():
            start(load_three(b - 1))

        @pl.when(b != at.seq)
        def _():
            from_owner(b).wait_recv()
        wait(load_three(b))
        wide, narrow = unpack_rows(proj[b].astype(f32), rows, tall)
        narrow = jnp.where(lane < tall, narrow, 0.0)
        wide16, narrow16 = wide.astype(b16), narrow.astype(b16)
        act16 = held16[lax.rem(b, 3)]
        g_act = (dot_of(wide16, w_proj[:, :rank], NT) + dot_of(narrow16[:, :tall], w_proj[:, rank:], NT)
                 + held[lax.rem(b, 3)])
        turned = jnp.concatenate([jnp.transpose(wide), jnp.transpose(narrow)[:tall]], axis=0).astype(b16)
        acc_proj[...] += jnp.dot(turned, act16, preferred_element_type=f32)
        pre = window[slot]
        s = jax.nn.sigmoid(pre)
        g_pre = g_act * s * (1.0 + pre * (1.0 - s))
        wider = jnp.concatenate([g_pre, ahead[0:8, :]], axis=0)
        ahead[0:8, :] = g_pre[0:8]
        accs[taps:taps + 1, :] += jnp.sum(g_pre, axis=0, keepdims=True)
        stream = three[slot, 0].astype(f32)
        g_stream = 0.0
        for j in range(taps):
            moved = wider[taps - 1 - j:taps - 1 - j + rows]
            g_stream = g_stream + pack[j:j + 1, :] * moved
            accs[j:j + 1, :] += jnp.sum(moved * stream, axis=0, keepdims=True)
        g16 = g_stream.astype(b16)
        g_gate = three[slot, 1]
        @pl.when(b == seq_count - 1)
        def _():
            weights.wait()
        if slots < seq_count:
            @pl.when(b + slots < seq_count)
            def _():
                wait_sent(b + slots)
        for m in range(0, model, lanes):
            cols = slice(m, m + lanes)
            g_normed = dot_of(g16, w_in[0, cols, :], NT) + dot_of(g_gate, w_in[1, cols, :], NT)
            box[:, cols] += jnp.sum(g_normed * nbuf[slot, :, cols].astype(f32), axis=0, keepdims=True)
            pbuf[kept(b), :, cols] = g_normed.astype(b16)

        @pl.when(b == at.seq)
        def _():
            mypart[...] = pbuf[kept(b)]

        @pl.when(at.x != lax.rem(b, at.nx))
        def _():
            for p in range(pieces):
                to_column(b, p).start()
        for m in range(0, model, 256):
            acc[m:m + 256, :] += dot_of(nbuf[slot, :, m:m + 256], g16, TN)

    def from_column(b, place, p):
        zb = b // at.nx
        return send(xbuf.at[zb, place, piece(p)], xbuf.at[zb, place, piece(p)], xs.at[0, p], xr.at[zb, place, p],
                    (at.seq, at.wt))

    def arrived(slot, p):
        return send(zbuf.at[slot, piece(p)], zbuf.at[slot, piece(p)], zs.at[0, p], zr.at[slot, p], (at.seq, at.wt))

    step = 16

    def add_column(b, p, base, store, sources):
        zb = b // at.nx
        for place in range(at.nx - 1):
            from_column(b, place, p).wait_recv()
        for slot, there in sources:
            @pl.when(there)
            def _():
                arrived(slot, p).wait_recv()
        for i in range(0, short, step):
            here = pl.ds(p * short + i, step)
            value = base(here).astype(f32)
            for place in range(at.nx - 1):
                value = value + xbuf[zb, place, here, :].astype(f32)
            for slot, there in sources:
                value = value + jnp.where(there, zbuf[slot, here, :].astype(f32), 0.0)
            store(here, value)

    def pass_block(b, hops):
        zb, xb = b // at.nx, lax.rem(b, at.nx)

        @pl.when((at.x == xb) & (((zb > at.z) & (at.z == hops)) | ((zb < at.z) & (at.nz - 1 - at.z == hops))))
        def _():
            def store(here, value):
                pbuf[kept(b), here, :] = value.astype(b16)
            for p in range(pieces):
                add_column(b, p, lambda here: pbuf[kept(b), here, :], store, [(zb, hops > 0)] if hops else [])

                @pl.when(zb > at.z)
                def _():
                    onward(b, p, False).start()

                @pl.when(zb < at.z)
                def _():
                    onward(b, p, True).start()

    def each(i, _):
        b = seq_count - 1 - i

        @pl.when(b >= 0)
        def _():
            adjoint_block(b)

        @pl.when((b + 1 >= 0) & (b + 1 < seq_count))
        def _():
            sum_block(b + 1)

        @pl.when((b + 2 >= 0) & (b + 2 < seq_count))
        def _():
            conv_block(b + 2)
        for hops in range(at.nz - 1):
            later = b + 3 + 2 * hops

            @pl.when((later >= 0) & (later < seq_count))
            def _():
                pass_block(later, hops)
        return 0

    segments = min(8, seq_count)
    for s in range(segments):
        lax.fori_loop(s * seq_count // segments, (s + 1) * seq_count // segments, each, 0)
        turn(tasks)
    lax.fori_loop(seq_count, seq_count + 2, each, 0)

    @pl.loop(0, seq_count)
    def _(i):
        for w in range(wt_count):
            high = late.shape[2]
            at_row = pl.multiple_of(i * (wt_count * high) + w * high, high)
            late[i, w] = acc[pl.ds(at_row, high), :].astype(b16)

    thin = width // wt_count
    for w in range(wt_count):
        cols = slice(w * thin, (w + 1) * thin)
        small[0, w, :rank] = acc_rate[:, cols]
        small[0, w, rank:rank + rank + tall] = acc_proj[:, cols]
        small[0, w, rank + rank + tall:] = accs[:, cols]
    box[...] = box[...] / gain[...]
    late_tasks.append(grads_task(at, late, *grad_bufs[2], stream_out, grad_sems[2][:4], grad_sems[2][4:], hold=4))
    late_tasks.append(reduce_block(at, small, *small_bufs, small_out, small_sems))
    turn(late_tasks)
    lax.fori_loop(seq_count + 2, seq_count + 3, each, 0)
    turn(late_tasks)
    late_tasks.append(all_sum(at, box, wbox, sbox, sum_sems))
    lax.fori_loop(seq_count + 3, seq_count + 3 + 2 * (at.nz - 2), each, 0)
    turn(late_tasks)
    turn(late_tasks)

    def emit(here, g):
        own_rows = own[here, :].astype(f32)
        inv = inverse[here, :]
        scaled = g * gain[...]
        mean = jnp.mean(scaled * own_rows, axis=-1, keepdims=True)
        tokens_out[here, :] = (g_own[here, :].astype(f32) + inv * scaled
                               - own_rows * (inv * inv * inv) * mean)

    def rest():
        for p in range(pieces):
            add_column(at.seq, p, lambda here: mypart[here, :], emit,
                       [(at.z, at.z > 0), (at.nz, at.z < at.nz - 1)])
            yield

    take_turns([rest()] + tasks + late_tasks)
    gain_out[...] = box[...]
    rate_out[...] = small_out[0, :rank, :]
    proj_out[...] = small_out[0, rank:rank + rank + tall, :]
    done = rank + rank + tall
    taps_out[...] = small_out[0, done:done + taps, :]
    bias_out[...] = small_out[0, done + taps:done + taps + 1, :]
    rbias_out[...] = small_out[0, done + taps + 1:done + taps + 2, :]
    skip_out[...] = small_out[0, done + taps + 2:done + taps + 3, :]

    @pl.loop(0, seq_count)
    def _(b):
        @pl.when(b != at.seq)
        def _():
            to_owner(b).wait_send()

    @pl.loop(0, slots)
    def _(b):
        wait_sent(b)
    for d in range(1, seq_count):
        to_all(d).wait_send()


def back(arrays, kq, rate_in, last, early, w_rate, w_proj, pack, own, g_own, inverse, gain, valid,
         seq_count, wt_count):
    gated = arrays[-2]
    w_in = arrays[-1]
    rows, model = own.shape
    width = gated.shape[-1]
    states = last.shape[0]
    tall = 2 * states
    rank = w_rate.shape[0]
    high = early[0].shape[-2]
    half = rows // 2
    nx = 1 << ((seq_count.bit_length() - 1) // 2)
    nz = seq_count // nx
    ny = wt_count // 2
    taps = pack.shape[0] - 4
    payload = (rank + tall * rows // 128, 128)
    block = (seq_count, high, width)
    lanes = model // wt_count
    small_rows = 2 * rank + tall + 8
    thin = width // wt_count
    small_block = (1, small_rows, width // wt_count)
    y_less = max(ny - 1, 1)
    vmem = pltpu.VMEM
    dma = pltpu.SemaphoreType.DMA

    def like(shape, dtype):
        return jax.ShapeDtypeStruct(shape, dtype)

    block_bufs = [vmem((ny,) + block, b16), vmem((y_less,) + block, b16), vmem((y_less,) + block, b16),
                  vmem(block, b16), vmem(block, b16)]
    small_bufs = [vmem((ny,) + small_block, f32), vmem((y_less,) + small_block, f32), vmem((y_less,) + small_block, f32)]
    return pl.pallas_call(
        functools.partial(back_kernel, seq_count, wt_count),
        in_specs=[ANY] * 12 + [IN_VMEM] * 13,
        out_specs=[IN_VMEM] * 11,
        out_shape=[like((rows, model), f32), like((high, 2 * seq_count * width), f32), like((high, seq_count * width), f32),
                   like((rank, thin), f32), like((rank + tall, thin), f32), like((taps, thin), f32), like((1, thin), f32),
                   like((1, thin), f32), like((1, thin), f32), like((rows, model), b16), like((1, model), f32)],
        scratch_shapes=[vmem((states, width), f32), vmem((states, width), f32), vmem((half, tall, 128), f32),
                        vmem((2, half, states, width), b16), vmem((half, tall, 128), f32),
                        vmem((rows, width), f32), vmem((rows, width), f32), vmem((tall, rows), f32),
                        vmem((2, 4, rows, width), f32), vmem((2, 2, rows, width), b16), vmem((2, rows, model), b16),
                        vmem((3, rows, width), f32), vmem((3, rows, width), b16), vmem((3, rows, width), f32),
                        vmem((8, width), f32),
                        vmem((seq_count,) + payload, b16), vmem((seq_count,) + payload, b16), vmem(payload, f32),
                        vmem((seq_count,) + payload, b16),
                        vmem((min(seq_count, 16), rows, model), b16), vmem((nz, nx - 1, rows, model), b16),
                        vmem((nz + 1, rows, model), b16), vmem((model, width), f32), vmem((rank, width), f32),
                        vmem((rank + tall, width), f32), vmem((seq_count, wt_count, high, width), b16),
                        vmem((1, wt_count) + small_block[1:], f32),
                        vmem(small_block, f32),
                        vmem((wt_count, seq_count, rows, width), b16), vmem((wt_count, rows, lanes), f32),
                        vmem((2, width, lanes), b16), vmem((rows, model), b16), vmem((wt_count, rows, lanes), b16),
                        vmem((1, model), f32), vmem((wt_count - 1, 1, model), f32), vmem((seq_count, 1, model), f32), vmem(w_in.shape, b16), vmem((wt_count, rows, lanes), b16)]
        + block_bufs * 3 + small_bufs
        + [dma((2,)), dma((2, 4)), dma((2, 3)), dma((2,)), dma((2,)), dma((2,))] + [dma((seq_count,))] * 4
        + [dma((min(seq_count, 16), 8)), dma((nz, nx - 1, 8)), dma((min(seq_count, 16), 8)), dma((nz + 1, 8)), dma((wt_count,)), dma((wt_count,))]
        + [dma((seq_count,))] * 2 + [dma((ny,))] * 4
        + ([dma((ny,))] * 4 + [dma((seq_count,))] * 2) * 3
        + [dma((ny,))] * 4 + [dma((wt_count - 1,))] * 2 + [dma((seq_count,))] * 2,
        compiler_params=pltpu.CompilerParams(collective_id=5, has_side_effects=True, vmem_limit_bytes=62 * MIB),
        name="back",
    )(*arrays, kq, rate_in, last, *early, w_rate, w_proj, pack, own, g_own, inverse, gain, valid)


def silu_parts(v):
    s = jax.nn.sigmoid(v)
    return v * s, s * (1.0 + v * (1.0 - s))


def on_device(
    tokens,
    lengths,
    norm_gain,
    in_weight,
    conv_taps,
    conv_bias,
    proj_weight,
    rate_weight,
    rate_bias,
    skip_gain,
    out_weight,
    cotangent,
):
    num_seqs, piece_len, model_width = tokens.shape
    inner_width = out_weight.shape[0]
    rate_rank = rate_weight.shape[0]
    states = (proj_weight.shape[1] - rate_rank) // 2
    conv_len = conv_taps.shape[0]
    seq_count = lax.axis_size("seq")
    wt_count = lax.axis_size("wt")
    length = piece_len * seq_count
    rows = num_seqs * length
    own_rows = num_seqs * piece_len
    width = inner_width // seq_count
    place = lax.axis_index("seq")

    own = tokens.reshape(own_rows, model_width)
    positions = place * piece_len + jnp.arange(piece_len, dtype=jnp.int32)
    valid = (positions[None, :] < lengths[:, None]).astype(f32).reshape(own_rows, 1)
    g_own16 = lax.optimization_barrier((cotangent.reshape(own_rows, model_width).astype(f32) * valid).astype(b16))
    pack = jnp.concatenate(
        [conv_taps] + [v[None] for v in (conv_bias, rate_bias, skip_gain, skip_gain)], 0).astype(f32)
    (normed, w_in, w_out, g_out, held, gate16, pre, stream16, act, scanned16, last, sig, u, key_query, projected,
     pack, w_rate, w_proj, inverse_rms, gain) = front(
        own, norm_gain.astype(f32).reshape(1, -1), in_weight, out_weight, pack, rate_weight, proj_weight, g_own16,
        states, width, seq_count, wt_count)
    normed = normed.reshape(rows, model_width)
    g_out = g_out.reshape(rows, model_width)
    w_in = w_in.reshape(2, model_width, width)
    inverse_rms = inverse_rms[:, :1]
    gain = gain.reshape(1, model_width)
    taps = pack[:conv_len]
    skip = pack[conv_len + 2][None]
    gate = gate16.astype(f32)
    rate_in = projected[:, :rate_rank]

    g_gated = jnp.einsum("td,id->ti", g_out, w_out, preferred_element_type=f32)
    gate_silu, gate_slope = silu_parts(gate)
    g_scanned = g_gated * gate_silu
    mixer = scanned16.astype(f32) + skip * act
    gated16 = (mixer * gate_silu).astype(b16)
    g_gate16 = (g_gated * mixer * gate_slope).astype(b16)
    part_out = jnp.einsum("td,ti->di", g_out, gated16, preferred_element_type=f32).astype(b16)
    part_gate = jnp.einsum("td,tk->dk", normed, g_gate16, preferred_element_type=f32).astype(b16)

    def by_owner(array):
        return array.reshape(array.shape[:-2] + (seq_count, wt_count, -1, width))

    (grad_tokens, inw_own, outw_own, ratew_own, projw_own, taps_own, cbias_own, rbias_own, skip_own, result,
     grad_gain) = back(
        (act, u, g_scanned, sig, pre, stream16, g_gate16, normed, held, out_weight,
         gated16.reshape(seq_count, own_rows, width), w_in),
        key_query, rate_in, last, (by_owner(part_gate), by_owner(part_out)), w_rate, w_proj, pack,
        own, g_own16, inverse_rms, gain, valid, seq_count, wt_count)
    result = result.reshape(tokens.shape)
    outw_own = outw_own.T
    projw_own = projw_own.T
    cbias_own, rbias_own, skip_own = cbias_own[0], rbias_own[0], skip_own[0]
    grad_tokens = grad_tokens.reshape(tokens.shape)
    owner = place * wt_count + lax.axis_index("wt")
    gain_own = lax.dynamic_slice_in_dim(grad_gain[0], owner * inw_own.shape[0], inw_own.shape[0], 0)
    return (
        result,
        grad_tokens,
        gain_own,
        inw_own,
        taps_own,
        cbias_own,
        projw_own,
        ratew_own,
        rbias_own,
        skip_own,
        outw_own,
    )


def solution(mesh):
    in_specs = (
        P("wt", "seq", None),
        P("wt"),
        P("wt"),
        P("wt", None),
        P(None, "wt"),
        P("wt"),
        P("wt", None),
        P(None, "wt"),
        P("wt"),
        P("wt"),
        P(None, "wt"),
        P("wt", "seq", None),
    )
    out_specs = (
        P("wt", "seq", None),
        P("wt", "seq", None),
        P(("seq", "wt")),
        P(("seq", "wt"), None),
        P(None, ("seq", "wt")),
        P(("seq", "wt")),
        P(("seq", "wt"), None),
        P(None, ("seq", "wt")),
        P(("seq", "wt")),
        P(("seq", "wt")),
        P(None, ("seq", "wt")),
    )
    return jax.shard_map(
        on_device, mesh=mesh, in_specs=in_specs, out_specs=out_specs, check_vma=False
    )
```
